256 devices in a mesh: space: 32 (over x_hi, z, core), vel: 8 (over y, x_lo).
Axes of the slice: x: 4 (x_hi: 2, x_lo: 2; x = x_hi * 2 + x_lo), y: 4, z: 8, core: 2. Of those that a mesh axis runs over, the one named last changes fastest.
Arguments:
- dist: float32 [128, 8, 8, 4096], P('space', None, None, 'vel'), may hold values from 0 to 5.5, as said below
- cell_type: int32 [128, 8, 8], replicated, may hold values from 0 to 3, as said below
- boundary: float32 [6], replicated, may hold values from 0.8 to 1.2
Outputs:
- renewed: float32 [128, 8, 8, 4096], P('space', None, None, 'vel')
The draws below stay inside these ranges and needn't reach their ends.
Inputs may be any that keep to these rules, and one draw needn't show every extreme that they name: `dist`: every entry is positive. `cell_type`: cells of kind 1 never lie on the grid's outer layer; kind 2 lies only in the plane x = 0 and kind 3 only in the plane x = 127, and both occur in every draw.
All inputs are finite; a program needn't handle non-finite values.
Results may differ from the reference program's by a relative error of at most 0.0003.
Values sent between devices are 32-bit elements; how exact they have to be, the bound alone decides.
A program may use at most 64 MiB of HBM per device.

```python
import math
import jax
import jax.numpy as jnp
from jax import lax

NODES = 16
VELOCITIES = 4096
CELLS_Y = 8
CELLS_Z = 8
STEPS = 2
CELLS_X = 128


VMAX = 5.0


def draw_dist(key, part):
    keys = jax.random.split(jax.random.fold_in(key, 101), 10)
    shape = (CELLS_X, CELLS_Y, CELLS_Z)
    density = jnp.exp(jax.random.uniform(keys[0], shape, jnp.float32, math.log(0.5), math.log(2.0)))
    stream = jax.random.uniform(keys[1], shape, jnp.float32, 0.2, 1.2)
    noise = 0.08 * jax.random.truncated_normal(keys[5], -3.0, 3.0, shape + (VELOCITIES,), jnp.float32)
    drift_y = jax.random.uniform(keys[2], shape, jnp.float32, -0.3, 0.3)
    drift_z = jax.random.uniform(keys[3], shape, jnp.float32, -0.3, 0.3)
    temper = jax.random.uniform(keys[4], shape, jnp.float32, 0.7, 1.4)
    second_temper = jax.random.uniform(keys[6], shape, jnp.float32, 0.7, 1.4)
    share = jax.random.uniform(keys[7], shape, jnp.float32, 0.1, 0.4)
    jump = jax.random.uniform(keys[8], shape + (3,), jnp.float32, -1.0, 1.0)
    number = jnp.arange(VELOCITIES, dtype=jnp.int32)
    spacing = 2.0 * VMAX / NODES
    along_x = ((number // (NODES * NODES)).astype(jnp.float32) + 0.5) * spacing - VMAX
    along_y = ((number // NODES % NODES).astype(jnp.float32) + 0.5) * spacing - VMAX
    along_z = ((number % NODES).astype(jnp.float32) + 0.5) * spacing - VMAX

    def maxwell(center_x, center_y, center_z, heat_level):
        square = (along_x - center_x[..., None]) ** 2 + (along_y - center_y[..., None]) ** 2 + (along_z - center_z[..., None]) ** 2
        amplitude = density / (heat_level * jnp.sqrt(heat_level))
        return amplitude[..., None] * jnp.exp(-square / (2.0 * heat_level[..., None]))
    first_part = maxwell(stream, drift_y, drift_z, temper)
    second_part = maxwell(stream + jump[..., 0], drift_y + jump[..., 1], drift_z + jump[..., 2], second_temper)
    mixed = (1.0 - share[..., None]) * first_part + share[..., None] * second_part
    return mixed * (1.0 + noise)


def draw_cell_type(key, part):
    keys = jax.random.split(jax.random.fold_in(key, 202), 3)
    radius_y = jax.random.randint(keys[0], (CELLS_X,), max(CELLS_Y // 4, 1), max(CELLS_Y // 2, 2))
    radius_z = jax.random.randint(keys[1], (CELLS_X,), max(CELLS_Z // 4, 1), max(CELLS_Z // 2, 2))
    plane = jnp.arange(CELLS_X, dtype=jnp.int32)[:, None, None]
    across = jnp.arange(CELLS_Y, dtype=jnp.int32)[None, :, None]
    height = jnp.arange(CELLS_Z, dtype=jnp.int32)[None, None, :]
    open_y = jnp.abs(2 * across - (CELLS_Y - 1)) < 2 * radius_y[:, None, None]
    open_z = jnp.abs(2 * height - (CELLS_Z - 1)) < 2 * radius_z[:, None, None]
    opening = open_y & open_z
    interior = (plane > 0) & (plane < CELLS_X - 1)
    obstacle = (jax.random.randint(keys[2], (CELLS_X, CELLS_Y, CELLS_Z), 0, 6) == 0) & interior
    kinds = jnp.where(opening & jnp.logical_not(obstacle), 1, 0)
    kinds = jnp.where(opening & (plane == 0), 2, kinds)
    kinds = jnp.where(opening & (plane == CELLS_X - 1), 3, kinds)
    return kinds.astype(jnp.int32)


def setup_inputs(seed: int = 0) -> dict:
    key_of = jax.random.split(jax.random.key(seed), 4)
    dist = draw_dist(jax.random.fold_in(key_of[3], 71), 0)
    cell_type = draw_cell_type(jax.random.fold_in(key_of[3], 71), 0)
    boundary = jnp.clip(jax.random.uniform(key_of[2], (6,), jnp.float32, 0.8, 1.2), 0.8, 1.2)
    return {"dist": dist, "cell_type": cell_type, "boundary": boundary}


PRANDTL = 2.0 / 3.0
OMEGA = 0.81
MU_REF = 0.1
DT = 0.1
HALF = 0.05
VMAX = 5.0
PRECISE = lax.Precision.HIGHEST

def speeds_of(start, count):
    number = start + jnp.arange(count, dtype=jnp.int32)
    spacing = 2.0 * VMAX / NODES
    digits = (number // (NODES * NODES), number // NODES % NODES, number % NODES)
    return tuple(((node_digit.astype(jnp.float32) + 0.5) * spacing - VMAX for node_digit in digits))

def node_weight():
    return (2.0 * VMAX / NODES) ** 3 / (2.0 * math.pi) ** 1.5

def offsets(velocity, speeds):
    shifted = tuple((speeds[component] - velocity[component][..., None] for component in range(3)))
    square = shifted[0] * shifted[0] + shifted[1] * shifted[1] + shifted[2] * shifted[2]
    return (shifted, square)

def maxwellian(density, velocity, temper, speeds):
    shifted, square = offsets(velocity, speeds)
    amplitude = density / (temper * jnp.sqrt(temper))
    return amplitude[..., None] * jnp.exp(-square / (2.0 * temper[..., None]))

def shakhov(density, velocity, temper, heat_flux, speeds):
    shifted, square = offsets(velocity, speeds)
    amplitude = density / (temper * jnp.sqrt(temper))
    maxwell_part = amplitude[..., None] * jnp.exp(-square / (2.0 * temper[..., None]))
    projected = shifted[0] * heat_flux[0][..., None] + shifted[1] * heat_flux[1][..., None] + shifted[2] * heat_flux[2][..., None]
    factor = (1.0 - PRANDTL) / (5.0 * density * temper * temper)
    return maxwell_part * (1.0 + factor[..., None] * projected * (square / temper[..., None] - 5.0))

def relaxation(density, temper):
    return MU_REF * jnp.exp(OMEGA * jnp.log(temper)) / (density * temper)

def plain_table(speeds, weight):
    square = speeds[0] * speeds[0] + speeds[1] * speeds[1] + speeds[2] * speeds[2]
    return weight * jnp.stack([jnp.ones_like(square), speeds[0], speeds[1], speeds[2], 0.5 * square])

def project(values, moment_table):
    return jnp.einsum('pyzv,mv->mpyz', values, moment_table, precision=PRECISE)

def primitives(totals):
    density = totals[0]
    velocity = tuple((totals[1 + component] / density for component in range(3)))
    speed_sq = velocity[0] * velocity[0] + velocity[1] * velocity[1] + velocity[2] * velocity[2]
    temper = (2.0 * totals[4] / density - speed_sq) / 3.0
    return (density, velocity, temper)

def heat_terms(values, velocity, speeds, weight):
    shifted, square = offsets(velocity, speeds)
    energy = 0.5 * weight * square * values
    return jnp.stack([lax.optimization_barrier(jnp.sum(shifted[component] * energy, axis=-1)) for component in range(3)])

def limited(ahead, behind):
    return 0.5 * (jnp.sign(ahead) + jnp.sign(behind)) * jnp.minimum(jnp.abs(ahead), jnp.abs(behind))

def reconstruct(values, kinds, speeds, cell, ghost):
    density, velocity, temper, heat_flux, tau = cell
    target = shakhov(density, velocity, temper, heat_flux, speeds)
    spread = 2.0 * tau[..., None]
    before = ((spread - HALF) * values + 3.0 * HALF * target) / (spread + DT)
    middle = before[1:-1]
    planes, across, height, nodes_here = middle.shape
    side_y = jnp.broadcast_to(ghost, (planes, 1, height, nodes_here))
    padded = jnp.concatenate([side_y, middle, side_y], axis=1)
    slope_y = limited(padded[:, 2:] - middle, middle - padded[:, :-2])
    side_z = jnp.broadcast_to(ghost, (planes, across, 1, nodes_here))
    padded = jnp.concatenate([side_z, middle, side_z], axis=2)
    slope_z = limited(padded[:, :, 2:] - middle, middle - padded[:, :, :-2])
    slope_x = limited(before[2:] - middle, middle - before[:-2])
    fluid = (kinds[1:-1] == 1)[..., None]
    slope_x = jnp.where(fluid, slope_x, 0.0)
    slope_y = jnp.where(fluid, slope_y, 0.0)
    slope_z = jnp.where(fluid, slope_z, 0.0)
    centre = middle - HALF * (speeds[0] * slope_x + speeds[1] * slope_y + speeds[2] * slope_z)
    face_x = jnp.where(speeds[0] > 0, (centre + 0.5 * slope_x)[:-1], (centre - 0.5 * slope_x)[1:])
    inner = centre[1:-1]
    upper_y = inner + 0.5 * slope_y[1:-1]
    lower_y = inner - 0.5 * slope_y[1:-1]
    side_y = jnp.broadcast_to(ghost, (planes - 2, 1, height, nodes_here))
    face_y = jnp.where(speeds[1] > 0, jnp.concatenate([side_y, upper_y], axis=1), jnp.concatenate([lower_y, side_y], axis=1))
    upper_z = inner + 0.5 * slope_z[1:-1]
    lower_z = inner - 0.5 * slope_z[1:-1]
    side_z = jnp.broadcast_to(ghost, (planes - 2, across, 1, nodes_here))
    face_z = jnp.where(speeds[2] > 0, jnp.concatenate([side_z, upper_z], axis=2), jnp.concatenate([lower_z, side_z], axis=2))
    return (before, (face_x, face_y, face_z))

def face_flux(face, state, speeds):
    density, velocity, temper, heat_flux = state
    tau = relaxation(density, temper)
    heat_flux = tuple((2.0 * tau * component / (2.0 * tau + HALF * PRANDTL) for component in heat_flux))
    target = shakhov(density, velocity, temper, heat_flux, speeds)
    spread = 2.0 * tau[..., None]
    return (spread * face + HALF * target) / (spread + HALF)

def renew(values, before, fluxes, kinds, speeds, cell, boundary):
    density = cell[0][2:-2]
    velocity = tuple((component[2:-2] for component in cell[1]))
    plus = (4.0 * before[2:-2] - values[2:-2]) / 3.0
    flux_x, flux_y, flux_z = fluxes
    change = speeds[0] * (flux_x[1:] - flux_x[:-1]) + speeds[1] * (flux_y[:, 1:] - flux_y[:, :-1]) + speeds[2] * (flux_z[:, :, 1:] - flux_z[:, :, :-1])
    fresh = plus - DT * change
    blank = jnp.zeros_like(density)
    inlet = maxwellian(boundary[0] + blank, (boundary[1] + blank, blank, blank), boundary[2] + blank, speeds)
    outlet = maxwellian(boundary[3] + blank, velocity, boundary[4] + blank, speeds)
    wall = maxwellian(density, (blank, blank, blank), boundary[5] + blank, speeds)
    kind = kinds[2:-2][..., None]
    return jnp.where(kind == 1, fresh, jnp.where(kind == 2, inlet, jnp.where(kind == 3, outlet, wall)))

def step(values, kinds, boundary):
    block = min(VELOCITIES, 512)
    count = VELOCITIES // block
    weight = node_weight()
    blank = jnp.zeros((), jnp.float32)
    ghost_all = maxwellian(boundary[3], (blank, blank, blank), boundary[5], speeds_of(0, VELOCITIES))
    ghost_planes = jnp.broadcast_to(ghost_all, (2, CELLS_Y, CELLS_Z, VELOCITIES))
    padded = jnp.concatenate([ghost_planes, values, ghost_planes], axis=0)
    kinds_pad = jnp.pad(kinds, ((2, 2), (0, 0), (0, 0)))
    numbers = jnp.arange(count, dtype=jnp.int32)

    def piece(number):
        start = number * block
        return (lax.dynamic_slice_in_dim(padded, start, block, 3), speeds_of(start, block))

    def cell_sum(number):
        portion, nodes = piece(number)
        return project(portion, plain_table(nodes, weight))
    density, velocity, temper = primitives(lax.optimization_barrier(jnp.sum(lax.map(cell_sum, numbers), axis=0)))

    def cell_heat(number):
        portion, nodes = piece(number)
        return heat_terms(portion, velocity, nodes, weight)
    heat_sum = lax.optimization_barrier(jnp.sum(lax.map(cell_heat, numbers), axis=0))
    tau = relaxation(density, temper)
    heat_flux = tuple((heat_sum[component] / (1.0 + DT * PRANDTL / (2.0 * tau)) for component in range(3)))
    cell = (density, velocity, temper, heat_flux, tau)

    def faces_of(number):
        portion, nodes = piece(number)
        ghost = lax.dynamic_slice_in_dim(ghost_all, number * block, block, 0)
        return (nodes, portion, reconstruct(portion, kinds_pad, nodes, cell, ghost))

    def face_sum(number):
        nodes, portion, rebuilt = faces_of(number)
        moment_table = plain_table(nodes, weight)
        return tuple((project(face, moment_table) for face in rebuilt[1]))
    states = [primitives(lax.optimization_barrier(jnp.sum(member, axis=0))) for member in lax.map(face_sum, numbers)]

    def face_heat(number):
        nodes, portion, rebuilt = faces_of(number)
        return tuple((heat_terms(face, state[1], nodes, weight) for face, state in zip(rebuilt[1], states)))
    flux_sums = [lax.optimization_barrier(jnp.sum(member, axis=0)) for member in lax.map(face_heat, numbers)]
    states = [state + ((flux_sum[0], flux_sum[1], flux_sum[2]),) for state, flux_sum in zip(states, flux_sums)]

    def renewed_block(number):
        nodes, portion, rebuilt = faces_of(number)
        fluxes = [face_flux(face, state, nodes) for face, state in zip(rebuilt[1], states)]
        return renew(portion, rebuilt[0], fluxes, kinds_pad, nodes, cell, boundary)
    blocks = lax.map(renewed_block, numbers)
    return jnp.moveaxis(blocks, 0, 3).reshape(CELLS_X, CELLS_Y, CELLS_Z, VELOCITIES)

def reference(dist, cell_type, boundary):
    values = dist
    for turn in range(STEPS):
        values = step(values, cell_type, boundary)
    return values
```

```python
import functools
import math

import jax
import jax.numpy as jnp
from jax import lax
from jax.experimental import pallas as pl
from jax.experimental.pallas import tpu as pltpu
from jax.sharding import PartitionSpec as P

MESH = pl.DeviceIdType.MESH
F32 = jnp.float32
BF16 = jnp.bfloat16

NODES = 16
STEPS = 2
PRANDTL = 2.0 / 3.0
DT = 0.1
HALF = 0.05
VMAX = 5.0
KAPPA = VMAX / NODES
WEIGHT = (2.0 * VMAX / NODES) ** 3 / (2.0 * math.pi) ** 1.5
LOG2E = math.log2(math.e)
LN_KAPPA2 = 2.0 * math.log(KAPPA)
TILES = 4
LANES = 128


def minmod(a, b):
    return jnp.maximum(jnp.minimum(a, b), 0.0) + jnp.minimum(jnp.maximum(a, b), 0.0)


def put_rows(c_ref, n, base, rows):
    for i, r in enumerate(rows):
        c_ref[base + i : base + i + 1, :n] = r


def expansion(c_ref, n, l_ref):
    c = c_ref[:, :n]
    hi = c.astype(BF16).astype(F32)
    rest = c - hi
    mid = rest.astype(BF16).astype(F32)
    low = rest - mid
    full = jnp.concatenate([hi, mid, low, jnp.zeros((8, n), F32)], axis=0)
    l_ref[:n, :] = full.T


def gauss_rows(nu, speed_sq, inv_theta):
    zero = jnp.zeros_like(inv_theta)
    c4 = (-0.5 * LOG2E) * inv_theta
    c1 = LOG2E * inv_theta
    return [c4 * speed_sq, c1 * nu[0], c1 * nu[1], c1 * nu[2], c4, c4, c4]


def target_rows(tot_ref, n, c_ref, width, cells):
    row = lambda i: tot_ref[i : i + 1, :n]
    m0 = row(0)
    inv = 1.0 / m0
    nu = [row(1) * inv, row(2) * inv, row(3) * inv]
    speed_sq = nu[0] * nu[0] + nu[1] * nu[1] + nu[2] * nu[2]
    sxx, syy, szz, sxy, sxz, syz = (row(i) for i in range(4, 10))
    trace = sxx + syy + szz
    theta = (trace * inv - speed_sq) * (1.0 / 3.0)
    inv_theta = 1.0 / theta
    dots = (
        sxx * nu[0] + sxy * nu[1] + sxz * nu[2],
        sxy * nu[0] + syy * nu[1] + syz * nu[2],
        sxz * nu[0] + syz * nu[1] + szz * nu[2],
    )
    density = WEIGHT * m0
    tau2 = 0.2 * jnp.exp(-0.19 * (jnp.log(theta) + LN_KAPPA2)) / density
    damp = tau2 / (tau2 + width * PRANDTL)
    scale = damp * inv * inv_theta * inv_theta * (1.0 / 30.0)
    heat = [
        scale
        * (
            row(10 + i)
            + row(13 + i)
            - 2.0 * dots[i]
            - nu[i] * trace
            + 2.0 * m0 * nu[i] * speed_sq
        )
        for i in range(3)
    ]
    if cells:
        spread = 1.0 / (tau2 + DT)
        keep = (tau2 - HALF) * spread
        give = (3.0 * HALF) * spread
    else:
        spread = 1.0 / (tau2 + HALF)
        keep = tau2 * spread
        give = HALF * spread
    amp = give * density * inv_theta * jnp.sqrt(inv_theta) * (KAPPA**-3)
    drift = heat[0] * nu[0] + heat[1] * nu[1] + heat[2] * nu[2]
    excess = speed_sq * inv_theta - 5.0
    ah = [amp * h for h in heat]
    ai = amp * inv_theta
    dt = ai * drift
    aih = [ai * h for h in heat]
    ae = excess
    put_rows(c_ref, n, 0, gauss_rows(nu, speed_sq, inv_theta))
    put_rows(
        c_ref,
        n,
        16,
        [
            amp - amp * drift * excess,
            ah[0] * ae + 2.0 * dt * nu[0],
            ah[1] * ae + 2.0 * dt * nu[1],
            ah[2] * ae + 2.0 * dt * nu[2],
            -2.0 * aih[0] * nu[0] - dt,
            -2.0 * aih[1] * nu[1] - dt,
            -2.0 * aih[2] * nu[2] - dt,
            -2.0 * (aih[0] * nu[1] + aih[1] * nu[0]),
            -2.0 * (aih[0] * nu[2] + aih[2] * nu[0]),
            -2.0 * (aih[1] * nu[2] + aih[2] * nu[1]),
            aih[0],
            aih[1],
            aih[2],
            aih[0],
            aih[1],
            aih[2],
            keep,
        ],
    )


def solid_rows(tot_ref, kind, bound, c_ref, n):
    row = lambda i: tot_ref[i : i + 1, 128 : 128 + n]
    m0 = row(0)
    inv = 1.0 / m0
    zero = jnp.zeros_like(m0)
    inlet, outlet = kind == 2.0, kind == 3.0
    density = jnp.where(inlet, bound(0) + zero, jnp.where(outlet, bound(3) + zero, WEIGHT * m0))
    temper = jnp.where(inlet, bound(2) + zero, jnp.where(outlet, bound(4) + zero, bound(5) + zero))
    nu = [
        jnp.where(
            inlet,
            (bound(1) * (1.0 / KAPPA) if i == 0 else 0.0) + zero,
            jnp.where(outlet, row(1 + i) * inv, zero),
        )
        for i in range(3)
    ]
    speed_sq = nu[0] * nu[0] + nu[1] * nu[1] + nu[2] * nu[2]
    inv_t = 1.0 / temper
    put_rows(c_ref, n, 0, gauss_rows(nu, speed_sq, inv_t * (KAPPA * KAPPA)))
    put_rows(c_ref, n, 32, [density * inv_t * jnp.sqrt(inv_t)])


def kernel(
    n_space,
    n_vel,
    dist,
    kinds,
    bound_ref,
    out,
    F,
    B,
    X,
    Y,
    Z,
    W,
    MX,
    Sc,
    Rc,
    Rl,
    Rr,
    Sf,
    Rf,
    tot,
    C,
    CM,
    Lc,
    Lm,
    Lf,
    TE,
    TP,
    TA,
    T16,
    kt,
    kb,
    kr,
    in_sem,
    kt_sem,
    halo_s,
    halo_r,
    cell_s,
    cell_r,
    left_s,
    left_r,
    right_s,
    right_r,
    face_s,
    face_r,
):
    s = lax.axis_index("space")
    v = lax.axis_index("vel")
    positive = v >= n_vel // 2
    last = n_space - 1
    total_planes = 4 * n_space
    bound = lambda i: bound_ref[i]
    place = lambda q: jnp.where(positive, q, 7 - q)

    load = pltpu.make_async_copy(dist, F.at[0, 2:6], in_sem)
    load.start()
    kind_loads = []
    for j in range(6):
        plane = jnp.clip(4 * s + (j - 1), 0, total_planes - 1)
        cp = pltpu.make_async_copy(kinds.at[plane], kt.at[j], kt_sem.at[j])
        cp.start()
        kind_loads.append(cp)

    barrier = pltpu.get_barrier_semaphore()
    for d in range(1, n_vel):
        pl.semaphore_signal(
            barrier, 1, device_id={"vel": lax.rem(v + d, n_vel)}, device_id_type=MESH
        )

    def greet(to):
        for d in range(n_vel):
            pl.semaphore_signal(
                barrier,
                1,
                device_id={"space": to, "vel": lax.rem(v + d, n_vel)},
                device_id_type=MESH,
            )

    pl.when(s > 0)(lambda: greet(s - 1))
    pl.when(s < last)(lambda: greet(s + 1))

    node = lax.broadcasted_iota(jnp.int32, (1, TILES * LANES), 1)
    nx = (4 * v - 15 + 2 * (node // 256)).astype(F32)
    ny = (2 * (node // 16 % 16) - 15).astype(F32)
    nz = (2 * (node % 16) - 15).astype(F32)
    square = nx * nx + ny * ny + nz * nz
    cubes = [nx * square, ny * square, nz * square]
    coarse = [c.astype(BF16).astype(F32) for c in cubes]
    rows = [jnp.ones_like(nx), nx, ny, nz, nx * nx, ny * ny, nz * nz, nx * ny, nx * nz, ny * nz]
    rows += coarse + [c - h for c, h in zip(cubes, coarse)]
    table = jnp.concatenate(rows, axis=0)
    z8 = jnp.zeros((8, TILES * LANES), F32)
    T16[...] = table.astype(BF16)
    TE[...] = jnp.concatenate([table, z8, z8, z8] * 3 + [z8], axis=0).astype(BF16)
    TP[...] = jnp.concatenate([z8, z8, table, z8] * 3 + [z8], axis=0).astype(BF16)
    line = lax.broadcasted_iota(jnp.int32, (128, LANES), 0)
    TA[...] = jnp.where(line % 40 == 32, 1.0, 0.0).astype(BF16)
    C[...] = jnp.zeros_like(C)
    CM[...] = jnp.zeros_like(CM)

    lane = lax.broadcasted_iota(jnp.int32, (8, LANES), 1)
    sub = lax.broadcasted_iota(jnp.int32, (8, LANES), 0)
    xi_x = [KAPPA * (4 * v - 15 + 2 * a).astype(F32) for a in range(2)]
    abs_x = [jnp.abs(x) for x in xi_x]
    xi_y = [KAPPA * (2 * (lane // 16 + 8 * b) - 15).astype(F32) for b in range(2)]
    xi_z = KAPPA * (2 * (lane % 16) - 15).astype(F32)
    up_z = lane % 16 >= 8

    def moments(values, cells):
        hi = values.astype(BF16)
        low = (values - hi.astype(F32)).astype(BF16)
        nt = (((1,), (1,)), ((), ()))
        t = T16[...]
        return lax.dot_general(t, hi, nt, preferred_element_type=F32) + lax.dot_general(
            t, low, nt, preferred_element_type=F32
        )

    def relax(l_rows, get, put):
        left = l_rows.astype(BF16)
        e = jnp.dot(left, TE[...], preferred_element_type=F32)
        p = jnp.dot(left, TP[...], preferred_element_type=F32)
        a = jnp.dot(left, TA[...], preferred_element_type=F32)
        for t in range(TILES):
            cut = slice(t * LANES, (t + 1) * LANES)
            put(t, a * get(t) + jnp.exp2(e[:, cut]) * p[:, cut])

    def peer_copies(src, dst, send, recv, lo, extra):
        return [
            pltpu.make_async_remote_copy(
                src,
                dst.at[d - lo],
                send.at[d - lo],
                recv.at[d - lo],
                device_id={**extra, "vel": lax.rem(v + d, n_vel)},
                device_id_type=MESH,
            )
            for d in range(lo, n_vel)
        ]

    def cell_copies(k):
        return peer_copies(Sc.at[k], Rc.at[k], cell_s.at[k], cell_r.at[k], 1, {})

    def right_copies(k):
        return peer_copies(
            Sc.at[k, :, 128:256], Rl.at[k], right_s.at[k], left_r.at[k], 0, {"space": s + 1}
        )

    def left_copies(k):
        return peer_copies(
            Sc.at[k, :, 0:128], Rr.at[k], left_s.at[k], right_r.at[k], 0, {"space": s - 1}
        )

    down = jnp.where(positive, s + 1, s - 1)
    upw = jnp.where(positive, s - 1, s + 1)
    has_down = jnp.where(positive, s < last, s > 0)
    has_up = jnp.where(positive, s > 0, s < last)

    def down_copies(k):
        near_src, far_src = place(5), place(4)
        near_dst, far_dst = place(1), place(0)
        return [
            pltpu.make_async_remote_copy(
                F.at[k, near_src],
                F.at[k, near_dst],
                halo_s.at[k, 0],
                halo_r.at[k, 0],
                device_id={"space": down},
                device_id_type=MESH,
            ),
            pltpu.make_async_remote_copy(
                F.at[k, far_src, 1:7],
                F.at[k, far_dst, 1:7],
                halo_s.at[k, 1],
                halo_r.at[k, 1],
                device_id={"space": down},
                device_id_type=MESH,
            ),
        ]

    def up_copies(k):
        return [
            pltpu.make_async_remote_copy(
                F.at[k, place(2), 1:7],
                F.at[k, place(6), 1:7],
                halo_s.at[k, 2],
                halo_r.at[k, 2],
                device_id={"space": upw},
                device_id_type=MESH,
            )
        ]

    def start(copies):
        for cp in copies:
            cp.start()

    def landed(copies):
        for cp in copies:
            cp.wait_recv()

    def left_free(copies):
        for cp in copies:
            cp.wait_send()

    def send_cells(k):
        start(cell_copies(k))
        pl.when(s < last)(lambda: start(right_copies(k)))
        pl.when(s > 0)(lambda: start(left_copies(k)))

    def send_halo(k):
        pl.when(has_down)(lambda: start(down_copies(k)))
        pl.when(has_up)(lambda: start(up_copies(k)))

    def face_copies(k, e):
        return peer_copies(Sf.at[k, e], Rf.at[k, e], face_s.at[k, e], face_r.at[k, e], 1, {})

    load.wait()
    Sc[0] = moments(F[0, 2:6].reshape(256, TILES * LANES), 256)

    inside = (s > 0) & (s < last)
    pl.when(inside)(lambda: pl.semaphore_wait(barrier, 3 * n_vel - 1))
    pl.when(jnp.logical_not(inside))(lambda: pl.semaphore_wait(barrier, 2 * n_vel - 1))
    send_halo(0)
    send_cells(0)

    for cp in kind_loads:
        cp.wait()
    tile8 = lax.broadcasted_iota(jnp.int32, (8, 8), 0) == lax.broadcasted_iota(
        jnp.int32, (8, 8), 1
    )
    for j in range(6):
        for y in range(8):
            line8 = jnp.broadcast_to(kt[j, y : y + 1, :].astype(F32), (8, 8))
            column = jnp.sum(jnp.where(tile8, line8, 0.0), axis=1, keepdims=True)
            kb[j, y] = jnp.broadcast_to(column, (8, LANES))
    for pair in range(2):
        gathered = jnp.zeros((8, LANES), F32)
        for half in range(2):
            for y in range(8):
                here = lane // 8 == half * 8 + y
                gathered = jnp.where(here, kb[1 + 2 * pair + half, y], gathered)
        gathered = jnp.where(lane % 8 == sub, gathered, 0.0)
        kr[0:1, pair * LANES : (pair + 1) * LANES] = jnp.sum(gathered, axis=0, keepdims=True)
    for j in range(6):
        for y in range(8):
            kb[j, y] = jnp.where(kb[j, y] == 1.0, 1.0, 0.0)

    def one_step(k):
        landed(cell_copies(k))
        sums = Sc[k]
        for d in range(n_vel - 1):
            sums = sums + Rc[k, d]
        tot[:, 128:384] = sums

        def from_left():
            landed(right_copies(k))
            part = Rl[k, 0]
            for d in range(1, n_vel):
                part = part + Rl[k, d]
            tot[:, 0:128] = part

        def from_right():
            landed(left_copies(k))
            part = Rr[k, 0]
            for d in range(1, n_vel):
                part = part + Rr[k, d]
            tot[:, 384:512] = part

        def no_left():
            tot[:, 0:128] = tot[:, 128:256]

        def no_right():
            tot[:, 384:512] = tot[:, 256:384]

        pl.when(s > 0)(from_left)
        pl.when(s == 0)(no_left)
        pl.when(s < last)(from_right)
        pl.when(s == last)(no_right)
        target_rows(tot, 512, C, DT, True)
        expansion(C, 512, Lc)

        pl.when(has_up)(lambda: landed(down_copies(k)))
        pl.when(has_down)(lambda: landed(up_copies(k)))

        def no_up():
            F[k, place(0)] = F[k, place(2)]
            F[k, place(1)] = F[k, place(2)]

        def no_down():
            F[k, place(6)] = F[k, place(5)]

        pl.when(jnp.logical_not(has_up))(no_up)
        pl.when(jnp.logical_not(has_down))(no_down)

        def before(q, carry):
            i = place(q)
            l_rows = Lc[pl.ds(pl.multiple_of(i * 64, 64), 64), :]

            def get(t):
                return F[k, i, :, :, t * LANES : (t + 1) * LANES].reshape(64, LANES)

            def put(t, value):
                B[i, :, :, t * LANES : (t + 1) * LANES] = value.reshape(8, 8, LANES)

            relax(l_rows, get, put)
            return carry

        lax.fori_loop(0, 7, before, 0)

        def upwind(q, across):
            i, im, ip = place(q), place(q - 1), place(q + 1)
            face = jnp.where(positive, q - 1, 5 - q)
            own = i - 2
            for y in range(1, 7):
                fluid = kb[i - 1, y]
                for t in range(TILES):
                    cut = slice(t * LANES, (t + 1) * LANES)
                    b = B[i, y, :, cut]
                    slope_x = minmod(B[ip, y, :, cut] - b, b - B[im, y, :, cut]) * fluid
                    slope_y = minmod(B[i, y + 1, :, cut] - b, b - B[i, y - 1, :, cut]) * fluid
                    ahead = pltpu.roll(b, 7, 0) - b
                    slope_z = minmod(ahead, pltpu.roll(ahead, 1, 0)) * fluid
                    centre = b - HALF * (
                        abs_x[t // 2] * slope_x + xi_y[t % 2] * slope_y + xi_z * slope_z
                    )
                    X[face, y - 1, :, cut] = centre + 0.5 * slope_x
                    if across:
                        if t % 2:
                            Y[own, y, :, cut] = centre + 0.5 * slope_y
                        else:
                            Y[own, y - 1, :, cut] = centre - 0.5 * slope_y
                        edge = centre + jnp.where(up_z, 0.5 * slope_z, -0.5 * slope_z)
                        Z[own, y - 1, :, cut] = jnp.where(up_z, edge, pltpu.roll(edge, 7, 0))
            if across:
                for t in range(TILES):
                    cut = slice(t * LANES, (t + 1) * LANES)
                    if t % 2:
                        Y[own, 0, :, cut] = B[i, 0, :, cut]
                    else:
                        Y[own, 6, :, cut] = B[i, 7, :, cut]

        upwind(1, False)

        def upwind_own(q, carry):
            upwind(q, True)
            return carry

        lax.fori_loop(2, 6, upwind_own, 0)

        for e, (faces, count) in enumerate(((X, 240), (Y, 224), (Z, 192))):
            Sf[k, e, :, :count] = moments(faces[...].reshape(count, TILES * LANES), count)
            start(face_copies(k, e))

        solid_rows(tot, kr[0:1, :], bound, CM, 256)
        expansion(CM, 256, Lm)
        target = F.at[1, 2:6] if k == 0 else out

        def solids(p, carry):
            left = Lm[pl.ds(pl.multiple_of(p * 64, 64), 64), :].astype(BF16)
            e = jnp.dot(left, TE[...], preferred_element_type=F32)
            a = jnp.dot(left, TA[...], preferred_element_type=F32)
            for t in range(TILES):
                cut = slice(t * LANES, (t + 1) * LANES)
                target[p, :, :, cut] = (a * jnp.exp2(e[:, cut])).reshape(8, 8, LANES)
            W[p] = (4.0 * B[p + 2, 1:7] - F[k, p + 2, 1:7]) * (1.0 / 3.0)
            return carry

        lax.fori_loop(0, 4, solids, 0)

        for e, (faces, parts, lines) in enumerate(((X, 5, 6), (Y, 4, 7), (Z, 4, 6))):
            landed(face_copies(k, e))
            sums = Sf[k, e]
            for d in range(n_vel - 1):
                sums = sums + Rf[k, e, d]
            tot[:, 0:256] = sums
            target_rows(tot, 256, C, HALF, False)
            expansion(C, 256, Lf)
            size = lines * 8

            def flux(i, carry, faces=faces, lines=lines, size=size):
                l_rows = Lf[pl.ds(pl.multiple_of(i * size, 8), size), :]

                def get(t):
                    return faces[i, :, :, t * LANES : (t + 1) * LANES].reshape(size, LANES)

                def put(t, value):
                    faces[i, :, :, t * LANES : (t + 1) * LANES] = value.reshape(lines, 8, LANES)

                relax(l_rows, get, put)
                return carry

            lax.fori_loop(0, parts, flux, 0)

        def renew(p, carry):
            for y in range(1, 7):
                fluid = kb[p + 1, y] == 1.0
                for t in range(TILES):
                    cut = slice(t * LANES, (t + 1) * LANES)
                    z = Z[p, y - 1, :, cut]
                    change = (
                        xi_x[t // 2] * (X[p + 1, y - 1, :, cut] - X[p, y - 1, :, cut])
                        + xi_y[t % 2] * (Y[p, y, :, cut] - Y[p, y - 1, :, cut])
                        + xi_z * (z - pltpu.roll(z, 1, 0))
                    )
                    fresh = W[p, y - 1, :, cut] - DT * change
                    target[p, y, :, cut] = jnp.where(fluid, fresh, target[p, y, :, cut])
            return carry

        lax.fori_loop(0, 4, renew, 0)

    one_step(0)
    send_halo(1)
    Sc[1] = moments(F[1, 2:6].reshape(256, TILES * LANES), 256)
    send_cells(1)
    one_step(1)

    for k in range(STEPS):
        left_free(cell_copies(k))
        pl.when(s < last)(lambda k=k: left_free(right_copies(k)))
        pl.when(s > 0)(lambda k=k: left_free(left_copies(k)))
        pl.when(has_down)(lambda k=k: left_free(down_copies(k)))
        pl.when(has_up)(lambda k=k: left_free(up_copies(k)))
        for e in range(3):
            left_free(face_copies(k, e))


def solution(mesh):
    n_space, n_vel = mesh.shape["space"], mesh.shape["vel"]
    vmem, dma = pltpu.VMEM, pltpu.SemaphoreType.DMA
    width = TILES * LANES

    def on_device(dist, cell_type, boundary):
        peers = n_vel - 1
        return pl.pallas_call(
            functools.partial(kernel, n_space, n_vel),
            out_shape=jax.ShapeDtypeStruct(dist.shape, F32),
            in_specs=[
                pl.BlockSpec(memory_space=pl.ANY),
                pl.BlockSpec(memory_space=pl.ANY),
                pl.BlockSpec(memory_space=pltpu.SMEM),
            ],
            out_specs=pl.BlockSpec(memory_space=pltpu.VMEM),
            scratch_shapes=[
                vmem((2, 8, 8, 8, width), F32),
                vmem((8, 8, 8, width), F32),
                vmem((5, 6, 8, width), F32),
                vmem((4, 7, 8, width), F32),
                vmem((4, 6, 8, width), F32),
                vmem((4, 6, 8, width), F32),
                vmem((8, LANES), F32),
                vmem((2, 16, 256), F32),
                vmem((2, peers, 16, 256), F32),
                vmem((2, n_vel, 16, 128), F32),
                vmem((2, n_vel, 16, 128), F32),
                vmem((2, 3, 16, 256), F32),
                vmem((2, 3, peers, 16, 256), F32),
                vmem((16, 512), F32),
                vmem((40, 512), F32),
                vmem((40, 256), F32),
                vmem((512, 128), F32),
                vmem((256, 128), F32),
                vmem((256, 128), F32),
                vmem((128, width), BF16),
                vmem((128, width), BF16),
                vmem((128, LANES), BF16),
                vmem((16, width), BF16),
                vmem((6, 8, 8), jnp.int32),
                vmem((6, 8, 8, LANES), F32),
                vmem((8, 256), F32),
                dma,
                dma((6,)),
                dma((2, 3)),
                dma((2, 3)),
                dma((2, peers)),
                dma((2, peers)),
                dma((2, n_vel)),
                dma((2, n_vel)),
                dma((2, n_vel)),
                dma((2, n_vel)),
                dma((2, 3, peers)),
                dma((2, 3, peers)),
            ],
            compiler_params=pltpu.CompilerParams(
                collective_id=0, has_side_effects=True, vmem_limit_bytes=40 * 2**20
            ),
        )(dist, cell_type, boundary)

    return jax.shard_map(
        on_device,
        mesh=mesh,
        in_specs=(P("space", None, None, "vel"), P(), P()),
        out_specs=P("space", None, None, "vel"),
        check_vma=False,
    )
```

```python
import functools
import math

import jax
import jax.numpy as jnp
from jax import lax
from jax.experimental import pallas as pl
from jax.experimental.pallas import tpu as pltpu
from jax.sharding import PartitionSpec as P

MESH = pl.DeviceIdType.MESH
F32 = jnp.float32
BF16 = jnp.bfloat16

NODES = 16
STEPS = 2
PRANDTL = 2.0 / 3.0
DT = 0.1
HALF = 0.05
VMAX = 5.0
KAPPA = VMAX / NODES
WEIGHT = (2.0 * VMAX / NODES) ** 3 / (2.0 * math.pi) ** 1.5
LOG2E = math.log2(math.e)
LN_KAPPA2 = 2.0 * math.log(KAPPA)
TILES = 4
LANES = 128

X_AT = (32, 38, 0, 44, 50)
Y_AT = (56, 6, 13, 63)
Z_AT = (70, 20, 26, 76)
INNER = 32
FACES = 82


def minmod(a, b):
    return jnp.maximum(jnp.minimum(a, b), 0.0) + jnp.minimum(jnp.maximum(a, b), 0.0)


def put_rows(c_ref, n, base, rows):
    for i, r in enumerate(rows):
        c_ref[base + i : base + i + 1, :n] = r


def expansion(c_ref, n, l_ref):
    c = c_ref[:, :n]
    hi = c.astype(BF16).astype(F32)
    rest = c - hi
    mid = rest.astype(BF16).astype(F32)
    low = rest - mid
    full = jnp.concatenate([hi, mid, low, jnp.zeros((8, n), F32)], axis=0)
    l_ref[:n, :] = full.T


def gauss_rows(nu, speed_sq, inv_theta):
    zero = jnp.zeros_like(inv_theta)
    c4 = (-0.5 * LOG2E) * inv_theta
    c1 = LOG2E * inv_theta
    return [c4 * speed_sq, c1 * nu[0], c1 * nu[1], c1 * nu[2], c4, c4, c4]


def target_rows(tot_ref, n, c_ref, width, cells):
    row = lambda i: tot_ref[i : i + 1, :n]
    m0 = row(0)
    inv = 1.0 / m0
    nu = [row(1) * inv, row(2) * inv, row(3) * inv]
    speed_sq = nu[0] * nu[0] + nu[1] * nu[1] + nu[2] * nu[2]
    sxx, syy, szz, sxy, sxz, syz = (row(i) for i in range(4, 10))
    trace = sxx + syy + szz
    theta = (trace * inv - speed_sq) * (1.0 / 3.0)
    inv_theta = 1.0 / theta
    dots = (
        sxx * nu[0] + sxy * nu[1] + sxz * nu[2],
        sxy * nu[0] + syy * nu[1] + syz * nu[2],
        sxz * nu[0] + syz * nu[1] + szz * nu[2],
    )
    density = WEIGHT * m0
    tau2 = 0.2 * jnp.exp(-0.19 * (jnp.log(theta) + LN_KAPPA2)) / density
    damp = tau2 / (tau2 + width * PRANDTL)
    scale = damp * inv * inv_theta * inv_theta * (1.0 / 30.0)
    heat = [
        scale
        * (
            row(10 + i)
            - 2.0 * dots[i]
            - nu[i] * trace
            + 2.0 * m0 * nu[i] * speed_sq
        )
        for i in range(3)
    ]
    if cells:
        spread = 1.0 / (tau2 + DT)
        keep = (tau2 - HALF) * spread
        give = (3.0 * HALF) * spread
    else:
        spread = 1.0 / (tau2 + HALF)
        keep = tau2 * spread
        give = HALF * spread
    amp = give * density * inv_theta * jnp.sqrt(inv_theta) * (KAPPA**-3)
    drift = heat[0] * nu[0] + heat[1] * nu[1] + heat[2] * nu[2]
    excess = speed_sq * inv_theta - 5.0
    ah = [amp * h for h in heat]
    ai = amp * inv_theta
    dt = ai * drift
    aih = [ai * h for h in heat]
    ae = excess
    put_rows(c_ref, n, 0, gauss_rows(nu, speed_sq, inv_theta))
    put_rows(
        c_ref,
        n,
        16,
        [
            amp - amp * drift * excess,
            ah[0] * ae + 2.0 * dt * nu[0],
            ah[1] * ae + 2.0 * dt * nu[1],
            ah[2] * ae + 2.0 * dt * nu[2],
            -2.0 * aih[0] * nu[0] - dt,
            -2.0 * aih[1] * nu[1] - dt,
            -2.0 * aih[2] * nu[2] - dt,
            -2.0 * (aih[0] * nu[1] + aih[1] * nu[0]),
            -2.0 * (aih[0] * nu[2] + aih[2] * nu[0]),
            -2.0 * (aih[1] * nu[2] + aih[2] * nu[1]),
            aih[0],
            aih[1],
            aih[2],
            aih[0],
            aih[1],
            aih[2],
            keep,
        ],
    )


def solid_rows(tot_ref, kind, bound, c_ref, n):
    row = lambda i: tot_ref[i : i + 1, :n]
    m0 = row(0)
    inv = 1.0 / m0
    zero = jnp.zeros_like(m0)
    inlet, outlet = kind == 2.0, kind == 3.0
    density = jnp.where(inlet, bound(0) + zero, jnp.where(outlet, bound(3) + zero, WEIGHT * m0))
    temper = jnp.where(inlet, bound(2) + zero, jnp.where(outlet, bound(4) + zero, bound(5) + zero))
    nu = [
        jnp.where(
            inlet,
            (bound(1) * (1.0 / KAPPA) if i == 0 else 0.0) + zero,
            jnp.where(outlet, row(1 + i) * inv, zero),
        )
        for i in range(3)
    ]
    speed_sq = nu[0] * nu[0] + nu[1] * nu[1] + nu[2] * nu[2]
    inv_t = 1.0 / temper
    put_rows(c_ref, n, 0, gauss_rows(nu, speed_sq, inv_t * (KAPPA * KAPPA)))
    put_rows(c_ref, n, 32, [density * inv_t * jnp.sqrt(inv_t)])


def kernel(
    n_space,
    n_vel,
    dist,
    kinds,
    bound_ref,
    out,
    F,
    B,
    G,
    W,
    O,
    Sc,
    Rc,
    Rl,
    Rr,
    Sf1,
    Rf1,
    Sf2,
    Rf2,
    totc,
    tote,
    totf,
    C,
    CM,
    Lc,
    Le,
    Lm,
    Lf,
    TE,
    TP,
    TA,
    T32,
    kt,
    kb,
    kr,
    in_sem,
    kt_sem,
    out_sem,
    halo_s,
    halo_r,
    cell_s,
    cell_r,
    left_s,
    left_r,
    right_s,
    right_r,
    face_s,
    face_r,
):
    s = lax.axis_index("space")
    v = lax.axis_index("vel")
    positive = v >= n_vel // 2
    last = n_space - 1
    bound = lambda i: bound_ref[i]
    place = lambda q: jnp.where(positive, q, 7 - q)

    barrier = pltpu.get_barrier_semaphore()
    for d in range(1, n_vel):
        pl.semaphore_signal(
            barrier, 1, device_id={"vel": lax.rem(v + d, n_vel)}, device_id_type=MESH
        )

    def greet(to):
        pl.semaphore_signal(barrier, 1, device_id={"space": to}, device_id_type=MESH)

    pl.when(s > 0)(lambda: greet(s - 1))
    pl.when(s < last)(lambda: greet(s + 1))

    load = pltpu.make_async_copy(dist, F.at[0, 2:6], in_sem)
    load.start()
    kind_load = pltpu.make_async_copy(kinds, kt, kt_sem)
    kind_load.start()

    node = lax.broadcasted_iota(jnp.int32, (1, TILES * LANES), 1)
    nx = (4 * v - 15 + 2 * (node // 256)).astype(F32)
    ny = (2 * (node // 16 % 16) - 15).astype(F32)
    nz = (2 * (node % 16) - 15).astype(F32)
    square = nx * nx + ny * ny + nz * nz
    cubes = [nx * square, ny * square, nz * square]
    coarse = [c.astype(BF16).astype(F32) for c in cubes]
    rows = [jnp.ones_like(nx), nx, ny, nz, nx * nx, ny * ny, nz * nz, nx * ny, nx * nz, ny * nz]
    rows += coarse + [c - h for c, h in zip(cubes, coarse)]
    table = jnp.concatenate(rows, axis=0)
    z8 = jnp.zeros((8, TILES * LANES), F32)
    z3 = jnp.zeros((3, TILES * LANES), F32)
    T32[...] = jnp.concatenate(
        rows[:13] + [z3, jnp.zeros((10, TILES * LANES), F32)] + rows[13:] + [z3], axis=0
    ).astype(BF16)
    TE[...] = jnp.concatenate([table, z8, z8, z8] * 3 + [z8], axis=0).astype(BF16)
    TP[...] = jnp.concatenate([z8, z8, table, z8] * 3 + [z8], axis=0).astype(BF16)
    line = lax.broadcasted_iota(jnp.int32, (128, LANES), 0)
    TA[...] = jnp.where(line % 40 == 32, 1.0, 0.0).astype(BF16)
    C[...] = jnp.zeros_like(C)
    CM[...] = jnp.zeros_like(CM)

    lane = lax.broadcasted_iota(jnp.int32, (8, LANES), 1)
    sub = lax.broadcasted_iota(jnp.int32, (8, LANES), 0)
    xi_x = [KAPPA * (4 * v - 15 + 2 * a).astype(F32) for a in range(2)]
    abs_x = [jnp.abs(x) for x in xi_x]
    xi_y = [KAPPA * (2 * (lane // 16 + 8 * b) - 15).astype(F32) for b in range(2)]
    xi_z = KAPPA * (2 * (lane % 16) - 15).astype(F32)
    up_z = lane % 16 >= 8

    def moments(values):
        hi = values.astype(BF16)
        low = (values - hi.astype(F32)).astype(BF16)
        nt = (((1,), (1,)), ((), ()))
        t = T32[...]
        both = lax.dot_general(t, hi, nt, preferred_element_type=F32) + lax.dot_general(
            t, low, nt, preferred_element_type=F32
        )
        return both[0:16] + both[16:32]

    def relax(l_rows, get, put):
        left = l_rows.astype(BF16)
        e = jnp.dot(left, TE[...], preferred_element_type=F32)
        p = jnp.dot(left, TP[...], preferred_element_type=F32)
        a = jnp.dot(left, TA[...], preferred_element_type=F32)
        for t in range(TILES):
            cut = slice(t * LANES, (t + 1) * LANES)
            put(t, a * get(t) + jnp.exp2(e[:, cut]) * p[:, cut])

    def peer_copies(src, dst, send, recv, lo, extra):
        return [
            pltpu.make_async_remote_copy(
                src,
                dst.at[d - lo],
                send.at[d - lo],
                recv.at[d - lo],
                device_id={**extra, "vel": lax.rem(v + d, n_vel)},
                device_id_type=MESH,
            )
            for d in range(lo, n_vel)
        ]

    def cell_copies(k):
        return peer_copies(
            Sc.at[k], Rc.at[k], cell_s.at[k], cell_r.at[k], 1, {}
        )

    def edge_copies(k, src, dst, send, recv, to):
        return [
            pltpu.make_async_remote_copy(
                totc.at[k, :, src],
                dst.at[k],
                send.at[k],
                recv.at[k],
                device_id=to,
                device_id_type=MESH,
            )
        ]

    def right_copies(k):
        return edge_copies(k, slice(128, 256), Rl, right_s, left_r, {"space": s + 1})

    def left_copies(k):
        return edge_copies(k, slice(0, 128), Rr, left_s, right_r, {"space": s - 1})

    down = jnp.where(positive, s + 1, s - 1)
    upw = jnp.where(positive, s - 1, s + 1)
    has_down = jnp.where(positive, s < last, s > 0)
    has_up = jnp.where(positive, s > 0, s < last)

    def halo_copy(k, which, src, dst, to):
        return pltpu.make_async_remote_copy(
            src,
            dst,
            halo_s.at[k, which],
            halo_r.at[k, which],
            device_id={"space": to},
            device_id_type=MESH,
        )

    def near_copies(k):
        return [halo_copy(k, 0, F.at[k, place(5)], F.at[k, place(1)], down)]

    def far_copies(k):
        return [halo_copy(k, 1, F.at[k, place(4), 1:7], F.at[k, place(0), 1:7], down)]

    def up_copies(k):
        return [halo_copy(k, 2, F.at[k, place(2), 1:7], F.at[k, place(6), 1:7], upw)]

    def start(copies):
        for cp in copies:
            cp.start()

    def landed(copies):
        for cp in copies:
            cp.wait_recv()

    def left_free(copies):
        for cp in copies:
            cp.wait_send()

    def send_edges(k):
        pl.when(s < last)(lambda: start(right_copies(k)))
        pl.when(s > 0)(lambda: start(left_copies(k)))

    def send_cells(k):
        Sc[k] = moments(F[k, 2:6].reshape(256, TILES * LANES))
        start(cell_copies(k))

    def send_near(k):
        pl.when(has_down)(lambda: start(near_copies(k)))
        pl.when(has_up)(lambda: start(up_copies(k)))

    def send_far(k):
        pl.when(has_down)(lambda: start(far_copies(k)))

    def face_copies(k, g):
        sf, rf = ((Sf1, Rf1), (Sf2, Rf2))[g]
        return peer_copies(
            sf.at[k], rf.at[k], face_s.at[k, g], face_r.at[k, g], 1, {}
        )

    load.wait()
    Sc[0] = moments(F[0, 2:6].reshape(256, TILES * LANES))

    inside = (s > 0) & (s < last)
    pl.when(inside)(lambda: pl.semaphore_wait(barrier, n_vel + 1))
    pl.when(jnp.logical_not(inside))(lambda: pl.semaphore_wait(barrier, n_vel))
    start(cell_copies(0))
    send_near(0)
    send_far(0)

    kind_load.wait()
    for j in range(6):
        plane = 4 * s + (j - 1)
        for y in range(8):
            column = jnp.sum(
                jnp.where(lane == plane, kt[y], 0).astype(F32), axis=1, keepdims=True
            )
            kb[j, y] = jnp.broadcast_to(column, (8, LANES))
    for pair in range(2):
        gathered = jnp.zeros((8, LANES), F32)
        for half in range(2):
            for y in range(8):
                here = lane // 8 == half * 8 + y
                gathered = jnp.where(here, kb[1 + 2 * pair + half, y], gathered)
        gathered = jnp.where(lane % 8 == sub, gathered, 0.0)
        kr[0:1, pair * LANES : (pair + 1) * LANES] = jnp.sum(gathered, axis=0, keepdims=True)
    for j in range(6):
        for y in range(8):
            kb[j, y] = jnp.where(kb[j, y] == 1.0, 1.0, 0.0)

    def one_step(k):
        def before(i, l_rows):
            def get(t):
                return F[k, i, :, :, t * LANES : (t + 1) * LANES].reshape(64, LANES)

            def put(t, value):
                B[i, :, :, t * LANES : (t + 1) * LANES] = value.reshape(8, 8, LANES)

            relax(l_rows, get, put)

        landed(cell_copies(k))
        sums = Sc[k]
        for d in range(n_vel - 1):
            sums = sums + Rc[k, d]
        totc[k] = sums
        send_edges(k)
        target_rows(totc.at[k], 256, C, DT, True)
        expansion(C, 256, Lc)
        for i in range(4):
            before(i + 2, Lc[i * 64 : i * 64 + 64, :])

        def upwind(q, across):
            i, im, ip = place(q), place(q - 1), place(q + 1)
            pick = lambda table: jnp.where(positive, table[0], table[1])
            x_at = pick((X_AT[q - 1], X_AT[5 - q]))
            if across:
                y_at = pick((Y_AT[q - 2], Y_AT[5 - q]))
                z_at = pick((Z_AT[q - 2], Z_AT[5 - q]))
            for y in range(1, 7):
                fluid = kb[i - 1, y]
                for t in range(TILES):
                    cut = slice(t * LANES, (t + 1) * LANES)
                    b = B[i, y, :, cut]
                    slope_x = minmod(B[ip, y, :, cut] - b, b - B[im, y, :, cut]) * fluid
                    slope_y = minmod(B[i, y + 1, :, cut] - b, b - B[i, y - 1, :, cut]) * fluid
                    ahead = pltpu.roll(b, 7, 0) - b
                    slope_z = minmod(ahead, pltpu.roll(ahead, 1, 0)) * fluid
                    centre = b - HALF * (
                        abs_x[t // 2] * slope_x + xi_y[t % 2] * slope_y + xi_z * slope_z
                    )
                    G[x_at + (y - 1), :, cut] = centre + 0.5 * slope_x
                    if across:
                        if t % 2:
                            G[y_at + y, :, cut] = centre + 0.5 * slope_y
                        else:
                            G[y_at + (y - 1), :, cut] = centre - 0.5 * slope_y
                        edge = centre + jnp.where(up_z, 0.5 * slope_z, -0.5 * slope_z)
                        G[z_at + (y - 1), :, cut] = jnp.where(up_z, edge, pltpu.roll(edge, 7, 0))
            if across:
                for t in range(TILES):
                    cut = slice(t * LANES, (t + 1) * LANES)
                    if t % 2:
                        G[y_at, :, cut] = B[i, 0, :, cut]
                    else:
                        G[y_at + 6, :, cut] = B[i, 7, :, cut]

        upwind(3, True)
        upwind(4, True)
        Sf1[k] = moments(G[0:INNER].reshape(INNER * 8, TILES * LANES))
        start(face_copies(k, 0))

        def total(copies, parts, cut):
            landed(copies)
            tote[:, cut] = parts[k]

        low, high = slice(0, 128), slice(128, 256)

        def no_left():
            tote[:, low] = totc[k, :, low]

        def no_right():
            tote[:, high] = totc[k, :, high]

        pl.when(s > 0)(lambda: total(right_copies(k), Rl, low))
        pl.when(s == 0)(no_left)
        pl.when(s < last)(lambda: total(left_copies(k), Rr, high))
        pl.when(s == last)(no_right)
        target_rows(tote, 256, C, DT, True)
        expansion(C, 256, Le)

        def up_landed():
            landed(near_copies(k))
            landed(far_copies(k))

        pl.when(has_up)(up_landed)
        pl.when(has_down)(lambda: landed(up_copies(k)))

        def no_up():
            F[k, place(0)] = F[k, place(2)]
            F[k, place(1)] = F[k, place(2)]

        def no_down():
            F[k, place(6)] = F[k, place(5)]

        pl.when(jnp.logical_not(has_up))(no_up)
        pl.when(jnp.logical_not(has_down))(no_down)
        for q, (ahead, behind) in ((0, (0, 192)), (1, (64, 128)), (6, (128, 64))):
            at = pl.multiple_of(jnp.where(positive, ahead, behind), 64)
            before(place(q), Le[pl.ds(at, 64), :])
        upwind(1, False)
        upwind(2, True)
        upwind(5, True)
        rest = (FACES - INNER) * 8
        Sf2[k, :, :rest] = moments(G[INNER:FACES].reshape(rest, TILES * LANES))
        start(face_copies(k, 1))

        target = F.at[1, 2:6] if k == 0 else O
        solid_rows(totc.at[k], kr[0:1, :], bound, CM, 256)
        expansion(CM, 256, Lm)
        for p in range(4):
            left = Lm[p * 64 : p * 64 + 64, :].astype(BF16)
            e = jnp.dot(left, TE[...], preferred_element_type=F32)
            a = jnp.dot(left, TA[...], preferred_element_type=F32)
            for t in range(TILES):
                cut = slice(t * LANES, (t + 1) * LANES)
                target[p, :, :, cut] = (a * jnp.exp2(e[:, cut])).reshape(8, 8, LANES)
            W[p] = (4.0 * B[p + 2, 1:7] - F[k, p + 2, 1:7]) * (1.0 / 3.0)

        for g, (sent, got, first, lines, block) in enumerate(
            ((Sf1, Rf1, 0, INNER, 8), (Sf2, Rf2, INNER, FACES - INNER, 10))
        ):
            landed(face_copies(k, g))
            sums = sent[k]
            for d in range(n_vel - 1):
                sums = sums + got[k, d]
            width = sums.shape[1]
            totf[:, :width] = sums
            target_rows(totf, width, C, HALF, False)
            expansion(C, width, Lf)
            size = block * 8
            for j in range(lines // block):
                at = first + j * block

                def get(t, at=at):
                    return G[at : at + block, :, t * LANES : (t + 1) * LANES].reshape(size, LANES)

                def put(t, value, at=at):
                    G[at : at + block, :, t * LANES : (t + 1) * LANES] = value.reshape(
                        block, 8, LANES
                    )

                relax(Lf[j * size : (j + 1) * size, :], get, put)

        for p in (3, 0, 2, 1):
            for y in range(1, 7):
                fluid = kb[p + 1, y] == 1.0
                for t in range(TILES):
                    cut = slice(t * LANES, (t + 1) * LANES)
                    z = G[Z_AT[p] + y - 1, :, cut]
                    change = (
                        xi_x[t // 2]
                        * (G[X_AT[p + 1] + y - 1, :, cut] - G[X_AT[p] + y - 1, :, cut])
                        + xi_y[t % 2] * (G[Y_AT[p] + y, :, cut] - G[Y_AT[p] + y - 1, :, cut])
                        + xi_z * (z - pltpu.roll(z, 1, 0))
                    )
                    fresh = W[p, y - 1, :, cut] - DT * change
                    target[p, y, :, cut] = jnp.where(fluid, fresh, target[p, y, :, cut])
            if k == STEPS - 1:
                pltpu.make_async_copy(O.at[p], out.at[p], out_sem.at[p]).start()
            elif p == 0:
                send_near(k + 1)
            elif p == 1:
                send_far(k + 1)

    one_step(0)
    send_cells(1)
    one_step(1)

    for k in range(STEPS):
        left_free(cell_copies(k))
        pl.when(s < last)(lambda k=k: left_free(right_copies(k)))
        pl.when(s > 0)(lambda k=k: left_free(left_copies(k)))
        pl.when(has_down)(lambda k=k: left_free(near_copies(k) + far_copies(k)))
        pl.when(has_up)(lambda k=k: left_free(up_copies(k)))
        for g in range(2):
            left_free(face_copies(k, g))
    for p in range(4):
        pltpu.make_async_copy(O.at[p], out.at[p], out_sem.at[p]).wait()


def solution(mesh):
    n_space, n_vel = mesh.shape["space"], mesh.shape["vel"]
    vmem, dma = pltpu.VMEM, pltpu.SemaphoreType.DMA
    width = TILES * LANES

    def on_device(dist, cell_type, boundary):
        peers = n_vel - 1
        return pl.pallas_call(
            functools.partial(kernel, n_space, n_vel),
            out_shape=jax.ShapeDtypeStruct(dist.shape, F32),
            in_specs=[
                pl.BlockSpec(memory_space=pltpu.HBM),
                pl.BlockSpec(memory_space=pltpu.HBM),
                pl.BlockSpec(memory_space=pltpu.SMEM),
            ],
            out_specs=pl.BlockSpec(memory_space=pl.ANY),
            scratch_shapes=[
                vmem((2, 8, 8, 8, width), F32),
                vmem((8, 8, 8, width), F32),
                vmem((FACES, 8, width), F32),
                vmem((4, 6, 8, width), F32),
                vmem((4, 8, 8, width), F32),
                vmem((2, 16, 256), F32),
                vmem((2, peers, 16, 256), F32),
                vmem((2, 16, 128), F32),
                vmem((2, 16, 128), F32),
                vmem((2, 16, 256), F32),
                vmem((2, peers, 16, 256), F32),
                vmem((2, 16, 512), F32),
                vmem((2, peers, 16, 512), F32),
                vmem((2, 16, 256), F32),
                vmem((16, 256), F32),
                vmem((16, 512), F32),
                vmem((40, 512), F32),
                vmem((40, 256), F32),
                vmem((256, 128), F32),
                vmem((256, 128), F32),
                vmem((256, 128), F32),
                vmem((512, 128), F32),
                vmem((128, width), BF16),
                vmem((128, width), BF16),
                vmem((128, LANES), BF16),
                vmem((32, width), BF16),
                vmem((8, 8, LANES), jnp.int32),
                vmem((6, 8, 8, LANES), F32),
                vmem((8, 256), F32),
                dma,
                dma,
                dma((4,)),
                dma((2, 3)),
                dma((2, 3)),
                dma((2, peers)),
                dma((2, peers)),
                dma((2,)),
                dma((2,)),
                dma((2,)),
                dma((2,)),
                dma((2, 2, peers)),
                dma((2, 2, peers)),
            ],
            compiler_params=pltpu.CompilerParams(
                collective_id=0, has_side_effects=True, vmem_limit_bytes=60 * 2**20
            ),
        )(dist, jnp.transpose(cell_type, (1, 2, 0)), boundary)

    return jax.shard_map(
        on_device,
        mesh=mesh,
        in_specs=(P("space", None, None, "vel"), P(), P()),
        out_specs=P("space", None, None, "vel"),
        check_vma=False,
    )
```

```python
import functools
import math

import jax
import jax.numpy as jnp
from jax import lax
from jax.experimental import pallas as pl
from jax.experimental.pallas import tpu as pltpu
from jax.sharding import PartitionSpec as P

MESH = pl.DeviceIdType.MESH
F32 = jnp.float32
BF16 = jnp.bfloat16

NODES = 16
STEPS = 2
PRANDTL = 2.0 / 3.0
DT = 0.1
HALF = 0.05
VMAX = 5.0
KAPPA = VMAX / NODES
WEIGHT = (2.0 * VMAX / NODES) ** 3 / (2.0 * math.pi) ** 1.5
LOG2E = math.log2(math.e)
LN_KAPPA2 = 2.0 * math.log(KAPPA)
TILES = 4
LANES = 128

FARTHEST_FIRST = (3, 5, 4, 1, 7, 2, 6)

X_AT = (32, 38, 0, 44, 50)
Y_AT = (56, 6, 13, 63)
Z_AT = (70, 20, 26, 76)
INNER = 32
FACES = 82


def minmod(a, b):
    return jnp.maximum(jnp.minimum(a, b), 0.0) + jnp.minimum(jnp.maximum(a, b), 0.0)


def put_rows(c_ref, n, base, rows):
    for i, r in enumerate(rows):
        c_ref[base + i : base + i + 1, :n] = r


def expansion(c_ref, n, l_ref):
    c = c_ref[:, :n]
    hi = c.astype(BF16).astype(F32)
    rest = c - hi
    mid = rest.astype(BF16).astype(F32)
    low = rest - mid
    full = jnp.concatenate([hi, mid, low, jnp.zeros((8, n), F32)], axis=0)
    l_ref[:n, :] = full.T


def gauss_rows(nu, speed_sq, inv_theta):
    zero = jnp.zeros_like(inv_theta)
    c4 = (-0.5 * LOG2E) * inv_theta
    c1 = LOG2E * inv_theta
    return [c4 * speed_sq, c1 * nu[0], c1 * nu[1], c1 * nu[2], c4, c4, c4]


def target_rows(tot_ref, n, c_ref, width, cells):
    row = lambda i: tot_ref[i : i + 1, :n]
    m0 = row(0)
    inv = 1.0 / m0
    nu = [row(1) * inv, row(2) * inv, row(3) * inv]
    speed_sq = nu[0] * nu[0] + nu[1] * nu[1] + nu[2] * nu[2]
    sxx, syy, szz, sxy, sxz, syz = (row(i) for i in range(4, 10))
    trace = sxx + syy + szz
    theta = (trace * inv - speed_sq) * (1.0 / 3.0)
    inv_theta = 1.0 / theta
    dots = (
        sxx * nu[0] + sxy * nu[1] + sxz * nu[2],
        sxy * nu[0] + syy * nu[1] + syz * nu[2],
        sxz * nu[0] + syz * nu[1] + szz * nu[2],
    )
    density = WEIGHT * m0
    tau2 = 0.2 * jnp.exp(-0.19 * (jnp.log(theta) + LN_KAPPA2)) / density
    damp = tau2 / (tau2 + width * PRANDTL)
    scale = damp * inv * inv_theta * inv_theta * (1.0 / 30.0)
    heat = [
        scale
        * (
            row(10 + i)
            - 2.0 * dots[i]
            - nu[i] * trace
            + 2.0 * m0 * nu[i] * speed_sq
        )
        for i in range(3)
    ]
    if cells:
        spread = 1.0 / (tau2 + DT)
        keep = (tau2 - HALF) * spread
        give = (3.0 * HALF) * spread
    else:
        spread = 1.0 / (tau2 + HALF)
        keep = tau2 * spread
        give = HALF * spread
    amp = give * density * inv_theta * jnp.sqrt(inv_theta) * (KAPPA**-3)
    drift = heat[0] * nu[0] + heat[1] * nu[1] + heat[2] * nu[2]
    excess = speed_sq * inv_theta - 5.0
    ah = [amp * h for h in heat]
    ai = amp * inv_theta
    dt = ai * drift
    aih = [ai * h for h in heat]
    ae = excess
    put_rows(c_ref, n, 0, gauss_rows(nu, speed_sq, inv_theta))
    put_rows(
        c_ref,
        n,
        16,
        [
            amp - amp * drift * excess,
            ah[0] * ae + 2.0 * dt * nu[0],
            ah[1] * ae + 2.0 * dt * nu[1],
            ah[2] * ae + 2.0 * dt * nu[2],
            -2.0 * aih[0] * nu[0] - dt,
            -2.0 * aih[1] * nu[1] - dt,
            -2.0 * aih[2] * nu[2] - dt,
            -2.0 * (aih[0] * nu[1] + aih[1] * nu[0]),
            -2.0 * (aih[0] * nu[2] + aih[2] * nu[0]),
            -2.0 * (aih[1] * nu[2] + aih[2] * nu[1]),
            aih[0],
            aih[1],
            aih[2],
            aih[0],
            aih[1],
            aih[2],
            keep,
        ],
    )


def solid_rows(tot_ref, kind, bound, c_ref, n):
    row = lambda i: tot_ref[i : i + 1, :n]
    m0 = row(0)
    inv = 1.0 / m0
    zero = jnp.zeros_like(m0)
    inlet, outlet = kind == 2.0, kind == 3.0
    density = jnp.where(inlet, bound(0) + zero, jnp.where(outlet, bound(3) + zero, WEIGHT * m0))
    temper = jnp.where(inlet, bound(2) + zero, jnp.where(outlet, bound(4) + zero, bound(5) + zero))
    nu = [
        jnp.where(
            inlet,
            (bound(1) * (1.0 / KAPPA) if i == 0 else 0.0) + zero,
            jnp.where(outlet, row(1 + i) * inv, zero),
        )
        for i in range(3)
    ]
    speed_sq = nu[0] * nu[0] + nu[1] * nu[1] + nu[2] * nu[2]
    inv_t = 1.0 / temper
    put_rows(c_ref, n, 0, gauss_rows(nu, speed_sq, inv_t * (KAPPA * KAPPA)))
    put_rows(c_ref, n, 32, [density * inv_t * jnp.sqrt(inv_t)])


def kernel(
    n_space,
    n_vel,
    dist,
    kinds,
    bound_any,
    out,
    F,
    B,
    G,
    W,
    O,
    Sc,
    Rc,
    Rl,
    Rr,
    Sf1,
    Rf1,
    Sf2,
    Rf2,
    totc,
    tote,
    totf,
    C,
    CM,
    Lc,
    Le,
    Lm,
    Lf,
    TE,
    TP,
    TA,
    T32,
    bound_ref,
    kt,
    kb,
    kr,
    in_sem,
    kt_sem,
    bound_sem,
    out_sem,
    halo_s,
    halo_r,
    cell_s,
    cell_r,
    left_s,
    left_r,
    right_s,
    right_r,
    face_s,
    face_r,
):
    s = lax.axis_index("space")
    v = lax.axis_index("vel")
    positive = v >= n_vel // 2
    last = n_space - 1
    bound = lambda i: bound_ref[i]
    place = lambda q: jnp.where(positive, q, 7 - q)

    barrier = pltpu.get_barrier_semaphore()
    for d in range(1, n_vel):
        pl.semaphore_signal(
            barrier, 1, device_id={"vel": lax.rem(v + d, n_vel)}, device_id_type=MESH
        )

    def greet(to):
        pl.semaphore_signal(barrier, 1, device_id={"space": to}, device_id_type=MESH)

    pl.when(s > 0)(lambda: greet(s - 1))
    pl.when(s < last)(lambda: greet(s + 1))

    load = pltpu.make_async_copy(dist, F.at[0, 2:6], in_sem)
    load.start()
    kind_load = pltpu.make_async_copy(kinds, kt, kt_sem)
    kind_load.start()
    bound_load = pltpu.make_async_copy(bound_any, bound_ref, bound_sem)
    bound_load.start()

    node = lax.broadcasted_iota(jnp.int32, (1, TILES * LANES), 1)
    nx = (4 * v - 15 + 2 * (node // 256)).astype(F32)
    ny = (2 * (node // 16 % 16) - 15).astype(F32)
    nz = (2 * (node % 16) - 15).astype(F32)
    square = nx * nx + ny * ny + nz * nz
    cubes = [nx * square, ny * square, nz * square]
    coarse = [c.astype(BF16).astype(F32) for c in cubes]
    rows = [jnp.ones_like(nx), nx, ny, nz, nx * nx, ny * ny, nz * nz, nx * ny, nx * nz, ny * nz]
    rows += coarse + [c - h for c, h in zip(cubes, coarse)]
    table = jnp.concatenate(rows, axis=0)
    z8 = jnp.zeros((8, TILES * LANES), F32)
    z3 = jnp.zeros((3, TILES * LANES), F32)
    T32[...] = jnp.concatenate(
        rows[:13] + [z3, jnp.zeros((10, TILES * LANES), F32)] + rows[13:] + [z3], axis=0
    ).astype(BF16)
    TE[...] = jnp.concatenate([table, z8, z8, z8] * 3 + [z8], axis=0).astype(BF16)
    TP[...] = jnp.concatenate([z8, z8, table, z8] * 3 + [z8], axis=0).astype(BF16)
    line = lax.broadcasted_iota(jnp.int32, (128, LANES), 0)
    TA[...] = jnp.where(line % 40 == 32, 1.0, 0.0).astype(BF16)
    C[...] = jnp.zeros_like(C)
    CM[...] = jnp.zeros_like(CM)

    lane = lax.broadcasted_iota(jnp.int32, (8, LANES), 1)
    sub = lax.broadcasted_iota(jnp.int32, (8, LANES), 0)
    xi_x = [KAPPA * (4 * v - 15 + 2 * a).astype(F32) for a in range(2)]
    abs_x = [jnp.abs(x) for x in xi_x]
    xi_y = [KAPPA * (2 * (lane // 16 + 8 * b) - 15).astype(F32) for b in range(2)]
    xi_z = KAPPA * (2 * (lane % 16) - 15).astype(F32)
    up_z = lane % 16 >= 8

    def moments(values):
        hi = values.astype(BF16)
        low = (values - hi.astype(F32)).astype(BF16)
        nt = (((1,), (1,)), ((), ()))
        t = T32[...]
        both = lax.dot_general(t, hi, nt, preferred_element_type=F32) + lax.dot_general(
            t, low, nt, preferred_element_type=F32
        )
        return both[0:16] + both[16:32]

    def relax(l_rows, get, put):
        left = l_rows.astype(BF16)
        e = jnp.dot(left, TE[...], preferred_element_type=F32)
        p = jnp.dot(left, TP[...], preferred_element_type=F32)
        a = jnp.dot(left, TA[...], preferred_element_type=F32)
        for t in range(TILES):
            cut = slice(t * LANES, (t + 1) * LANES)
            put(t, a * get(t) + jnp.exp2(e[:, cut]) * p[:, cut])

    def peer_copies(src, dst, send, recv):
        return [
            pltpu.make_async_remote_copy(
                src,
                dst.at[d - 1],
                send.at[d - 1],
                recv.at[d - 1],
                device_id={"vel": lax.rem(v + d, n_vel)},
                device_id_type=MESH,
            )
            for d in FARTHEST_FIRST
        ]

    def cell_copies(k):
        return peer_copies(
            Sc.at[k], Rc.at[k], cell_s.at[k], cell_r.at[k]
        )

    def edge_copies(k, src, dst, send, recv, to):
        return [
            pltpu.make_async_remote_copy(
                totc.at[k, :, src],
                dst.at[k],
                send.at[k],
                recv.at[k],
                device_id=to,
                device_id_type=MESH,
            )
        ]

    def right_copies(k):
        return edge_copies(k, slice(128, 256), Rl, right_s, left_r, {"space": s + 1})

    def left_copies(k):
        return edge_copies(k, slice(0, 128), Rr, left_s, right_r, {"space": s - 1})

    down = jnp.where(positive, s + 1, s - 1)
    upw = jnp.where(positive, s - 1, s + 1)
    has_down = jnp.where(positive, s < last, s > 0)
    has_up = jnp.where(positive, s > 0, s < last)

    def halo_copy(k, which, src, dst, to):
        return pltpu.make_async_remote_copy(
            src,
            dst,
            halo_s.at[k, which],
            halo_r.at[k, which],
            device_id={"space": to},
            device_id_type=MESH,
        )

    def near_copies(k):
        return [halo_copy(k, 0, F.at[k, place(5)], F.at[k, place(1)], down)]

    def far_copies(k):
        return [halo_copy(k, 1, F.at[k, place(4), 1:7], F.at[k, place(0), 1:7], down)]

    def up_copies(k):
        return [halo_copy(k, 2, F.at[k, place(2), 1:7], F.at[k, place(6), 1:7], upw)]

    def start(copies):
        for cp in copies:
            cp.start()

    def landed(copies):
        for cp in copies:
            cp.wait_recv()

    def left_free(copies):
        for cp in copies:
            cp.wait_send()

    def send_edges(k):
        pl.when(s < last)(lambda: start(right_copies(k)))
        pl.when(s > 0)(lambda: start(left_copies(k)))

    def send_cells(k):
        Sc[k] = moments(F[k, 2:6].reshape(256, TILES * LANES))
        start(cell_copies(k))

    def send_near(k):
        pl.when(has_down)(lambda: start(near_copies(k)))
        pl.when(has_up)(lambda: start(up_copies(k)))

    def send_far(k):
        pl.when(has_down)(lambda: start(far_copies(k)))

    def face_copies(k, g):
        sf, rf = ((Sf1, Rf1), (Sf2, Rf2))[g]
        return peer_copies(
            sf.at[k], rf.at[k], face_s.at[k, g], face_r.at[k, g]
        )

    load.wait()
    Sc[0] = moments(F[0, 2:6].reshape(256, TILES * LANES))

    inside = (s > 0) & (s < last)
    pl.when(inside)(lambda: pl.semaphore_wait(barrier, n_vel + 1))
    pl.when(jnp.logical_not(inside))(lambda: pl.semaphore_wait(barrier, n_vel))
    start(cell_copies(0))
    send_near(0)
    send_far(0)

    kind_load.wait()
    bound_load.wait()
    for j in range(6):
        plane = 4 * s + (j - 1)
        for y in range(8):
            column = jnp.sum(
                jnp.where(lane == plane, kt[y], 0).astype(F32), axis=1, keepdims=True
            )
            kb[j, y] = jnp.broadcast_to(column, (8, LANES))
    for pair in range(2):
        gathered = jnp.zeros((8, LANES), F32)
        for half in range(2):
            for y in range(8):
                here = lane // 8 == half * 8 + y
                gathered = jnp.where(here, kb[1 + 2 * pair + half, y], gathered)
        gathered = jnp.where(lane % 8 == sub, gathered, 0.0)
        kr[0:1, pair * LANES : (pair + 1) * LANES] = jnp.sum(gathered, axis=0, keepdims=True)
    for j in range(6):
        for y in range(8):
            kb[j, y] = jnp.where(kb[j, y] == 1.0, 1.0, 0.0)

    def one_step(k):
        def before(i, l_rows):
            def get(t):
                return F[k, i, :, :, t * LANES : (t + 1) * LANES].reshape(64, LANES)

            def put(t, value):
                B[i, :, :, t * LANES : (t + 1) * LANES] = value.reshape(8, 8, LANES)

            relax(l_rows, get, put)

        landed(cell_copies(k))
        sums = Sc[k]
        for d in range(n_vel - 1):
            sums = sums + Rc[k, d]
        totc[k] = sums
        send_edges(k)
        target_rows(totc.at[k], 256, C, DT, True)
        expansion(C, 256, Lc)
        for i in range(4):
            before(i + 2, Lc[i * 64 : i * 64 + 64, :])

        def upwind(q, across):
            i, im, ip = place(q), place(q - 1), place(q + 1)
            pick = lambda table: jnp.where(positive, table[0], table[1])
            x_at = pick((X_AT[q - 1], X_AT[5 - q]))
            if across:
                y_at = pick((Y_AT[q - 2], Y_AT[5 - q]))
                z_at = pick((Z_AT[q - 2], Z_AT[5 - q]))
            for y in range(1, 7):
                fluid = kb[i - 1, y]
                for t in range(TILES):
                    cut = slice(t * LANES, (t + 1) * LANES)
                    b = B[i, y, :, cut]
                    slope_x = minmod(B[ip, y, :, cut] - b, b - B[im, y, :, cut]) * fluid
                    slope_y = minmod(B[i, y + 1, :, cut] - b, b - B[i, y - 1, :, cut]) * fluid
                    ahead = pltpu.roll(b, 7, 0) - b
                    slope_z = minmod(ahead, pltpu.roll(ahead, 1, 0)) * fluid
                    centre = b - HALF * (
                        abs_x[t // 2] * slope_x + xi_y[t % 2] * slope_y + xi_z * slope_z
                    )
                    G[x_at + (y - 1), :, cut] = centre + 0.5 * slope_x
                    if across:
                        if t % 2:
                            G[y_at + y, :, cut] = centre + 0.5 * slope_y
                        else:
                            G[y_at + (y - 1), :, cut] = centre - 0.5 * slope_y
                        edge = centre + jnp.where(up_z, 0.5 * slope_z, -0.5 * slope_z)
                        G[z_at + (y - 1), :, cut] = jnp.where(up_z, edge, pltpu.roll(edge, 7, 0))
            if across:
                for t in range(TILES):
                    cut = slice(t * LANES, (t + 1) * LANES)
                    if t % 2:
                        G[y_at, :, cut] = B[i, 0, :, cut]
                    else:
                        G[y_at + 6, :, cut] = B[i, 7, :, cut]

        upwind(3, True)
        upwind(4, True)
        Sf1[k] = moments(G[0:INNER].reshape(INNER * 8, TILES * LANES))
        start(face_copies(k, 0))

        def total(copies, parts, cut):
            landed(copies)
            tote[:, cut] = parts[k]

        low, high = slice(0, 128), slice(128, 256)

        def no_left():
            tote[:, low] = totc[k, :, low]

        def no_right():
            tote[:, high] = totc[k, :, high]

        pl.when(s > 0)(lambda: total(right_copies(k), Rl, low))
        pl.when(s == 0)(no_left)
        pl.when(s < last)(lambda: total(left_copies(k), Rr, high))
        pl.when(s == last)(no_right)
        target_rows(tote, 256, C, DT, True)
        expansion(C, 256, Le)

        def up_landed():
            landed(near_copies(k))
            landed(far_copies(k))

        pl.when(has_up)(up_landed)
        pl.when(has_down)(lambda: landed(up_copies(k)))

        def no_up():
            F[k, place(0)] = F[k, place(2)]
            F[k, place(1)] = F[k, place(2)]

        def no_down():
            F[k, place(6)] = F[k, place(5)]

        pl.when(jnp.logical_not(has_up))(no_up)
        pl.when(jnp.logical_not(has_down))(no_down)
        for q, (ahead, behind) in ((0, (0, 192)), (1, (64, 128)), (6, (128, 64))):
            at = pl.multiple_of(jnp.where(positive, ahead, behind), 64)
            before(place(q), Le[pl.ds(at, 64), :])
        upwind(1, False)
        upwind(2, True)
        upwind(5, True)
        rest = (FACES - INNER) * 8
        Sf2[k, :, :rest] = moments(G[INNER:FACES].reshape(rest, TILES * LANES))
        start(face_copies(k, 1))

        target = F.at[1, 2:6] if k == 0 else O
        solid_rows(totc.at[k], kr[0:1, :], bound, CM, 256)
        expansion(CM, 256, Lm)
        for p in range(4):
            left = Lm[p * 64 : p * 64 + 64, :].astype(BF16)
            e = jnp.dot(left, TE[...], preferred_element_type=F32)
            a = jnp.dot(left, TA[...], preferred_element_type=F32)
            for t in range(TILES):
                cut = slice(t * LANES, (t + 1) * LANES)
                target[p, :, :, cut] = (a * jnp.exp2(e[:, cut])).reshape(8, 8, LANES)
            W[p] = (4.0 * B[p + 2, 1:7] - F[k, p + 2, 1:7]) * (1.0 / 3.0)

        for g, (sent, got, first, lines, block) in enumerate(
            ((Sf1, Rf1, 0, INNER, 8), (Sf2, Rf2, INNER, FACES - INNER, 10))
        ):
            landed(face_copies(k, g))
            sums = sent[k]
            for d in range(n_vel - 1):
                sums = sums + got[k, d]
            width = sums.shape[1]
            totf[:, :width] = sums
            target_rows(totf, width, C, HALF, False)
            expansion(C, width, Lf)
            size = block * 8
            for j in range(lines // block):
                at = first + j * block

                def get(t, at=at):
                    return G[at : at + block, :, t * LANES : (t + 1) * LANES].reshape(size, LANES)

                def put(t, value, at=at):
                    G[at : at + block, :, t * LANES : (t + 1) * LANES] = value.reshape(
                        block, 8, LANES
                    )

                relax(Lf[j * size : (j + 1) * size, :], get, put)

        for p in (3, 0, 2, 1):
            for y in range(1, 7):
                fluid = kb[p + 1, y] == 1.0
                for t in range(TILES):
                    cut = slice(t * LANES, (t + 1) * LANES)
                    z = G[Z_AT[p] + y - 1, :, cut]
                    change = (
                        xi_x[t // 2]
                        * (G[X_AT[p + 1] + y - 1, :, cut] - G[X_AT[p] + y - 1, :, cut])
                        + xi_y[t % 2] * (G[Y_AT[p] + y, :, cut] - G[Y_AT[p] + y - 1, :, cut])
                        + xi_z * (z - pltpu.roll(z, 1, 0))
                    )
                    fresh = W[p, y - 1, :, cut] - DT * change
                    target[p, y, :, cut] = jnp.where(fluid, fresh, target[p, y, :, cut])
            if k == STEPS - 1:
                pltpu.make_async_copy(O.at[p], out.at[p], out_sem.at[p]).start()
            elif p == 0:
                send_near(k + 1)
            elif p == 1:
                send_far(k + 1)

    one_step(0)
    send_cells(1)
    one_step(1)

    for k in range(STEPS):
        left_free(cell_copies(k))
        pl.when(s < last)(lambda k=k: left_free(right_copies(k)))
        pl.when(s > 0)(lambda k=k: left_free(left_copies(k)))
        pl.when(has_down)(lambda k=k: left_free(near_copies(k) + far_copies(k)))
        pl.when(has_up)(lambda k=k: left_free(up_copies(k)))
        for g in range(2):
            left_free(face_copies(k, g))
    for p in range(4):
        pltpu.make_async_copy(O.at[p], out.at[p], out_sem.at[p]).wait()


def solution(mesh):
    n_space, n_vel = mesh.shape["space"], mesh.shape["vel"]
    vmem, dma = pltpu.VMEM, pltpu.SemaphoreType.DMA
    width = TILES * LANES

    def on_device(dist, cell_type, boundary):
        peers = n_vel - 1
        return pl.pallas_call(
            functools.partial(kernel, n_space, n_vel),
            out_shape=jax.ShapeDtypeStruct(dist.shape, F32),
            in_specs=[
                pl.BlockSpec(memory_space=pltpu.HBM),
                pl.BlockSpec(memory_space=pltpu.HBM),
                pl.BlockSpec(memory_space=pl.ANY),
            ],
            out_specs=pl.BlockSpec(memory_space=pl.ANY),
            scratch_shapes=[
                vmem((2, 8, 8, 8, width), F32),
                vmem((8, 8, 8, width), F32),
                vmem((FACES, 8, width), F32),
                vmem((4, 6, 8, width), F32),
                vmem((4, 8, 8, width), F32),
                vmem((2, 16, 256), F32),
                vmem((2, peers, 16, 256), F32),
                vmem((2, 16, 128), F32),
                vmem((2, 16, 128), F32),
                vmem((2, 16, 256), F32),
                vmem((2, peers, 16, 256), F32),
                vmem((2, 16, 512), F32),
                vmem((2, peers, 16, 512), F32),
                vmem((2, 16, 256), F32),
                vmem((16, 256), F32),
                vmem((16, 512), F32),
                vmem((40, 512), F32),
                vmem((40, 256), F32),
                vmem((256, 128), F32),
                vmem((256, 128), F32),
                vmem((256, 128), F32),
                vmem((512, 128), F32),
                vmem((128, width), BF16),
                vmem((128, width), BF16),
                vmem((128, LANES), BF16),
                vmem((32, width), BF16),
                pltpu.SMEM((6,), F32),
                vmem((8, 8, LANES), jnp.int32),
                vmem((6, 8, 8, LANES), F32),
                vmem((8, 256), F32),
                dma,
                dma,
                dma,
                dma((4,)),
                dma((2, 3)),
                dma((2, 3)),
                dma((2, peers)),
                dma((2, peers)),
                dma((2,)),
                dma((2,)),
                dma((2,)),
                dma((2,)),
                dma((2, 2, peers)),
                dma((2, 2, peers)),
            ],
            compiler_params=pltpu.CompilerParams(
                collective_id=0, has_side_effects=True, vmem_limit_bytes=60 * 2**20
            ),
        )(dist, jnp.transpose(cell_type, (1, 2, 0)), boundary)

    return jax.shard_map(
        on_device,
        mesh=mesh,
        in_specs=(P("space", None, None, "vel"), P(), P()),
        out_specs=P("space", None, None, "vel"),
        check_vma=False,
    )
```

```python
import functools
import math

import jax
import jax.numpy as jnp
from jax import lax
from jax.experimental import pallas as pl
from jax.experimental.pallas import tpu as pltpu
from jax.sharding import PartitionSpec as P

MESH = pl.DeviceIdType.MESH
F32 = jnp.float32
BF16 = jnp.bfloat16

NODES = 16
STEPS = 2
PRANDTL = 2.0 / 3.0
DT = 0.1
HALF = 0.05
VMAX = 5.0
KAPPA = VMAX / NODES
WEIGHT = (2.0 * VMAX / NODES) ** 3 / (2.0 * math.pi) ** 1.5
LOG2E = math.log2(math.e)
LN_KAPPA2 = 2.0 * math.log(KAPPA)
TILES = 4
LANES = 128

FARTHEST_FIRST = (3, 5, 4, 1, 7, 2, 6)

X_AT = (32, 38, 0, 44, 50)
Y_AT = (56, 6, 13, 63)
Z_AT = (70, 20, 26, 76)
INNER = 32
FACES = 82
WIDE = 384


def minmod(a, b):
    return jnp.maximum(jnp.minimum(a, b), 0.0) + jnp.minimum(jnp.maximum(a, b), 0.0)


def put_rows(c_ref, n, base, rows):
    for i, r in enumerate(rows):
        c_ref[base + i : base + i + 1, :n] = r


def expansion(c_ref, n, l_ref):
    c = c_ref[:, :n]
    hi = c.astype(BF16).astype(F32)
    rest = c - hi
    mid = rest.astype(BF16).astype(F32)
    low = rest - mid
    full = jnp.concatenate([hi, mid, low, jnp.zeros((8, n), F32)], axis=0)
    l_ref[:n, :] = full.T


def gauss_rows(nu, speed_sq, inv_theta):
    zero = jnp.zeros_like(inv_theta)
    c4 = (-0.5 * LOG2E) * inv_theta
    c1 = LOG2E * inv_theta
    return [c4 * speed_sq, c1 * nu[0], c1 * nu[1], c1 * nu[2], c4, c4, c4]


def target_rows(tot_ref, n, c_ref, width, cells):
    row = lambda i: tot_ref[i : i + 1, :n]
    m0 = row(0)
    inv = 1.0 / m0
    nu = [row(1) * inv, row(2) * inv, row(3) * inv]
    speed_sq = nu[0] * nu[0] + nu[1] * nu[1] + nu[2] * nu[2]
    sxx, syy, szz, sxy, sxz, syz = (row(i) for i in range(4, 10))
    trace = sxx + syy + szz
    theta = (trace * inv - speed_sq) * (1.0 / 3.0)
    inv_theta = 1.0 / theta
    dots = (
        sxx * nu[0] + sxy * nu[1] + sxz * nu[2],
        sxy * nu[0] + syy * nu[1] + syz * nu[2],
        sxz * nu[0] + syz * nu[1] + szz * nu[2],
    )
    density = WEIGHT * m0
    tau2 = 0.2 * jnp.exp(-0.19 * (jnp.log(theta) + LN_KAPPA2)) / density
    damp = tau2 / (tau2 + width * PRANDTL)
    scale = damp * inv * inv_theta * inv_theta * (1.0 / 30.0)
    heat = [
        scale
        * (
            row(10 + i)
            - 2.0 * dots[i]
            - nu[i] * trace
            + 2.0 * m0 * nu[i] * speed_sq
        )
        for i in range(3)
    ]
    if cells:
        spread = 1.0 / (tau2 + DT)
        keep = (tau2 - HALF) * spread
        give = (3.0 * HALF) * spread
    else:
        spread = 1.0 / (tau2 + HALF)
        keep = tau2 * spread
        give = HALF * spread
    amp = give * density * inv_theta * jnp.sqrt(inv_theta) * (KAPPA**-3)
    drift = heat[0] * nu[0] + heat[1] * nu[1] + heat[2] * nu[2]
    excess = speed_sq * inv_theta - 5.0
    ah = [amp * h for h in heat]
    ai = amp * inv_theta
    dt = ai * drift
    aih = [ai * h for h in heat]
    ae = excess
    put_rows(c_ref, n, 0, gauss_rows(nu, speed_sq, inv_theta))
    put_rows(
        c_ref,
        n,
        16,
        [
            amp - amp * drift * excess,
            ah[0] * ae + 2.0 * dt * nu[0],
            ah[1] * ae + 2.0 * dt * nu[1],
            ah[2] * ae + 2.0 * dt * nu[2],
            -2.0 * aih[0] * nu[0] - dt,
            -2.0 * aih[1] * nu[1] - dt,
            -2.0 * aih[2] * nu[2] - dt,
            -2.0 * (aih[0] * nu[1] + aih[1] * nu[0]),
            -2.0 * (aih[0] * nu[2] + aih[2] * nu[0]),
            -2.0 * (aih[1] * nu[2] + aih[2] * nu[1]),
            aih[0],
            aih[1],
            aih[2],
            aih[0],
            aih[1],
            aih[2],
            keep,
        ],
    )


def solid_rows(tot_ref, kind, bound, c_ref, n):
    row = lambda i: tot_ref[i : i + 1, :n]
    m0 = row(0)
    inv = 1.0 / m0
    zero = jnp.zeros_like(m0)
    inlet, outlet = kind == 2.0, kind == 3.0
    density = jnp.where(inlet, bound(0) + zero, jnp.where(outlet, bound(3) + zero, WEIGHT * m0))
    temper = jnp.where(inlet, bound(2) + zero, jnp.where(outlet, bound(4) + zero, bound(5) + zero))
    nu = [
        jnp.where(
            inlet,
            (bound(1) * (1.0 / KAPPA) if i == 0 else 0.0) + zero,
            jnp.where(outlet, row(1 + i) * inv, zero),
        )
        for i in range(3)
    ]
    speed_sq = nu[0] * nu[0] + nu[1] * nu[1] + nu[2] * nu[2]
    inv_t = 1.0 / temper
    put_rows(c_ref, n, 0, gauss_rows(nu, speed_sq, inv_t * (KAPPA * KAPPA)))
    put_rows(c_ref, n, 32, [density * inv_t * jnp.sqrt(inv_t)])


def kernel(
    n_space,
    n_vel,
    dist,
    kinds,
    bound_any,
    out,
    F,
    B,
    G,
    W,
    O,
    Sc,
    Rc,
    Rl,
    Rr,
    Sf1,
    Rf1,
    Sf2,
    Rf2,
    totc,
    tote,
    totf,
    C,
    CM,
    Lc,
    Le,
    Lm,
    Lf,
    TE,
    TP,
    TA,
    T32,
    bound_ref,
    kt,
    kb,
    kr,
    in_sem,
    kt_sem,
    bound_sem,
    out_sem,
    halo_s,
    halo_r,
    cell_s,
    cell_r,
    left_s,
    left_r,
    right_s,
    right_r,
    face_s,
    face_r,
):
    s = lax.axis_index("space")
    v = lax.axis_index("vel")
    positive = v >= n_vel // 2
    last = n_space - 1
    bound = lambda i: bound_ref[i]
    place = lambda q: jnp.where(positive, q, 7 - q)

    barrier = pltpu.get_barrier_semaphore()
    def greet(to):
        pl.semaphore_signal(barrier, 1, device_id={"space": to}, device_id_type=MESH)

    pl.when(s > 0)(lambda: greet(s - 1))
    pl.when(s < last)(lambda: greet(s + 1))
    for d in FARTHEST_FIRST:
        pl.semaphore_signal(
            barrier, 1, device_id={"vel": lax.rem(v + d, n_vel)}, device_id_type=MESH
        )

    load = pltpu.make_async_copy(dist, F.at[0, 2:6], in_sem)
    load.start()
    kind_load = pltpu.make_async_copy(kinds, kt, kt_sem)
    kind_load.start()
    bound_load = pltpu.make_async_copy(bound_any, bound_ref, bound_sem)
    bound_load.start()

    node = lax.broadcasted_iota(jnp.int32, (1, TILES * LANES), 1)
    nx = (4 * v - 15 + 2 * (node // 256)).astype(F32)
    ny = (2 * (node // 16 % 16) - 15).astype(F32)
    nz = (2 * (node % 16) - 15).astype(F32)
    square = nx * nx + ny * ny + nz * nz
    cubes = [nx * square, ny * square, nz * square]
    coarse = [c.astype(BF16).astype(F32) for c in cubes]
    rows = [jnp.ones_like(nx), nx, ny, nz, nx * nx, ny * ny, nz * nz, nx * ny, nx * nz, ny * nz]
    rows += coarse + [c - h for c, h in zip(cubes, coarse)]
    table = jnp.concatenate(rows, axis=0)
    z8 = jnp.zeros((8, TILES * LANES), F32)
    z3 = jnp.zeros((3, TILES * LANES), F32)
    T32[...] = jnp.concatenate(
        rows[:13] + [z3, jnp.zeros((10, TILES * LANES), F32)] + rows[13:] + [z3], axis=0
    ).astype(BF16)
    TE[...] = jnp.concatenate([table, z8, z8, z8] * 3 + [z8], axis=0).astype(BF16)
    TP[...] = jnp.concatenate([z8, z8, table, z8] * 3 + [z8], axis=0).astype(BF16)
    line = lax.broadcasted_iota(jnp.int32, (128, LANES), 0)
    TA[...] = jnp.where(line % 40 == 32, 1.0, 0.0).astype(BF16)
    C[...] = jnp.zeros_like(C)
    CM[...] = jnp.zeros_like(CM)

    lane = lax.broadcasted_iota(jnp.int32, (8, LANES), 1)
    sub = lax.broadcasted_iota(jnp.int32, (8, LANES), 0)
    xi_x = [KAPPA * (4 * v - 15 + 2 * a).astype(F32) for a in range(2)]
    abs_x = [jnp.abs(x) for x in xi_x]
    xi_y = [KAPPA * (2 * (lane // 16 + 8 * b) - 15).astype(F32) for b in range(2)]
    xi_z = KAPPA * (2 * (lane % 16) - 15).astype(F32)
    up_z = lane % 16 >= 8

    def moments(values):
        hi = values.astype(BF16)
        low = (values - hi.astype(F32)).astype(BF16)
        nt = (((1,), (1,)), ((), ()))
        t = T32[...]
        both = lax.dot_general(t, hi, nt, preferred_element_type=F32) + lax.dot_general(
            t, low, nt, preferred_element_type=F32
        )
        return both[0:16] + both[16:32]

    def relax(l_rows, get, put):
        left = l_rows.astype(BF16)
        e = jnp.dot(left, TE[...], preferred_element_type=F32)
        p = jnp.dot(left, TP[...], preferred_element_type=F32)
        a = jnp.dot(left, TA[...], preferred_element_type=F32)
        for t in range(TILES):
            cut = slice(t * LANES, (t + 1) * LANES)
            put(t, a * get(t) + jnp.exp2(e[:, cut]) * p[:, cut])

    def peer_copies(src, dst, send, recv):
        return [
            pltpu.make_async_remote_copy(
                src,
                dst.at[d - 1],
                send.at[d - 1],
                recv.at[d - 1],
                device_id={"vel": lax.rem(v + d, n_vel)},
                device_id_type=MESH,
            )
            for d in FARTHEST_FIRST
        ]

    def cell_copies(k):
        return peer_copies(
            Sc.at[k], Rc.at[k], cell_s.at[k], cell_r.at[k]
        )

    def edge_copies(k, src, dst, send, recv, to):
        return [
            pltpu.make_async_remote_copy(
                totc.at[k, :, src],
                dst.at[k],
                send.at[k],
                recv.at[k],
                device_id=to,
                device_id_type=MESH,
            )
        ]

    def right_copies(k):
        return edge_copies(k, slice(128, 256), Rl, right_s, left_r, {"space": s + 1})

    def left_copies(k):
        return edge_copies(k, slice(0, 128), Rr, left_s, right_r, {"space": s - 1})

    down = jnp.where(positive, s + 1, s - 1)
    upw = jnp.where(positive, s - 1, s + 1)
    has_down = jnp.where(positive, s < last, s > 0)
    has_up = jnp.where(positive, s > 0, s < last)

    def halo_copy(k, which, src, dst, to):
        return pltpu.make_async_remote_copy(
            src,
            dst,
            halo_s.at[k, which],
            halo_r.at[k, which],
            device_id={"space": to},
            device_id_type=MESH,
        )

    def near_copies(k):
        return [halo_copy(k, 0, F.at[k, place(5)], F.at[k, place(1)], down)]

    def far_copies(k):
        return [halo_copy(k, 1, F.at[k, place(4), 1:7], F.at[k, place(0), 1:7], down)]

    def up_copies(k):
        return [halo_copy(k, 2, F.at[k, place(2), 1:7], F.at[k, place(6), 1:7], upw)]

    def start(copies):
        for cp in copies:
            cp.start()

    def landed(copies):
        for cp in copies:
            cp.wait_recv()

    def left_free(copies):
        for cp in copies:
            cp.wait_send()

    def send_edges(k):
        pl.when(s < last)(lambda: start(right_copies(k)))
        pl.when(s > 0)(lambda: start(left_copies(k)))

    def send_cells(k):
        Sc[k] = moments(F[k, 2:6].reshape(256, TILES * LANES))
        start(cell_copies(k))

    def send_near(k):
        pl.when(has_down)(lambda: start(near_copies(k)))
        pl.when(has_up)(lambda: start(up_copies(k)))

    def send_far(k):
        pl.when(has_down)(lambda: start(far_copies(k)))

    def face_copies(k, g):
        sf, rf = ((Sf1, Rf1), (Sf2, Rf2))[g]
        return peer_copies(
            sf.at[k], rf.at[k], face_s.at[k, g], face_r.at[k, g]
        )

    load.wait()
    Sc[0] = moments(F[0, 2:6].reshape(256, TILES * LANES))

    inside = (s > 0) & (s < last)
    pl.when(inside)(lambda: pl.semaphore_wait(barrier, n_vel + 1))
    pl.when(jnp.logical_not(inside))(lambda: pl.semaphore_wait(barrier, n_vel))
    start(cell_copies(0))
    send_near(0)
    send_far(0)

    kind_load.wait()
    bound_load.wait()
    for j in range(6):
        plane = 4 * s + (j - 1)
        for y in range(8):
            column = jnp.sum(
                jnp.where(lane == plane, kt[y], 0).astype(F32), axis=1, keepdims=True
            )
            kb[j, y] = jnp.broadcast_to(column, (8, LANES))
    for pair in range(2):
        gathered = jnp.zeros((8, LANES), F32)
        for half in range(2):
            for y in range(8):
                here = lane // 8 == half * 8 + y
                gathered = jnp.where(here, kb[1 + 2 * pair + half, y], gathered)
        gathered = jnp.where(lane % 8 == sub, gathered, 0.0)
        kr[0:1, pair * LANES : (pair + 1) * LANES] = jnp.sum(gathered, axis=0, keepdims=True)
    for j in range(6):
        for y in range(8):
            kb[j, y] = jnp.where(kb[j, y] == 1.0, 1.0, 0.0)

    def one_step(k):
        def before(i, l_rows):
            def get(t):
                return F[k, i, :, :, t * LANES : (t + 1) * LANES].reshape(64, LANES)

            def put(t, value):
                B[i, :, :, t * LANES : (t + 1) * LANES] = value.reshape(8, 8, LANES)

            relax(l_rows, get, put)

        landed(cell_copies(k))
        sums = Sc[k]
        for d in range(n_vel - 1):
            sums = sums + Rc[k, d]
        totc[k] = sums
        send_edges(k)
        target_rows(totc.at[k], 256, C, DT, True)
        expansion(C, 256, Lc)
        for i in range(4):
            before(i + 2, Lc[i * 64 : i * 64 + 64, :])

        def upwind(q, across):
            i, im, ip = place(q), place(q - 1), place(q + 1)
            pick = lambda table: jnp.where(positive, table[0], table[1])
            x_at = pick((X_AT[q - 1], X_AT[5 - q]))
            if across:
                y_at = pick((Y_AT[q - 2], Y_AT[5 - q]))
                z_at = pick((Z_AT[q - 2], Z_AT[5 - q]))
            for y in range(1, 7):
                fluid = kb[i - 1, y]
                for t in range(TILES):
                    cut = slice(t * LANES, (t + 1) * LANES)
                    b = B[i, y, :, cut]
                    slope_x = minmod(B[ip, y, :, cut] - b, b - B[im, y, :, cut]) * fluid
                    slope_y = minmod(B[i, y + 1, :, cut] - b, b - B[i, y - 1, :, cut]) * fluid
                    ahead = pltpu.roll(b, 7, 0) - b
                    slope_z = minmod(ahead, pltpu.roll(ahead, 1, 0)) * fluid
                    centre = b - HALF * (
                        abs_x[t // 2] * slope_x + xi_y[t % 2] * slope_y + xi_z * slope_z
                    )
                    G[x_at + (y - 1), :, cut] = centre + 0.5 * slope_x
                    if across:
                        if t % 2:
                            G[y_at + y, :, cut] = centre + 0.5 * slope_y
                        else:
                            G[y_at + (y - 1), :, cut] = centre - 0.5 * slope_y
                        edge = centre + jnp.where(up_z, 0.5 * slope_z, -0.5 * slope_z)
                        G[z_at + (y - 1), :, cut] = jnp.where(up_z, edge, pltpu.roll(edge, 7, 0))
            if across:
                for t in range(TILES):
                    cut = slice(t * LANES, (t + 1) * LANES)
                    if t % 2:
                        G[y_at, :, cut] = B[i, 0, :, cut]
                    else:
                        G[y_at + 6, :, cut] = B[i, 7, :, cut]

        upwind(3, True)
        upwind(4, True)
        Sf1[k] = moments(G[0:INNER].reshape(INNER * 8, TILES * LANES))
        start(face_copies(k, 0))

        def total(copies, parts, cut):
            landed(copies)
            tote[:, cut] = parts[k]

        low, high = slice(0, 128), slice(128, 256)

        def no_left():
            tote[:, low] = totc[k, :, low]

        def no_right():
            tote[:, high] = totc[k, :, high]

        pl.when(s > 0)(lambda: total(right_copies(k), Rl, low))
        pl.when(s == 0)(no_left)
        pl.when(s < last)(lambda: total(left_copies(k), Rr, high))
        pl.when(s == last)(no_right)
        target_rows(tote, 256, C, DT, True)
        expansion(C, 256, Le)

        def up_landed():
            landed(near_copies(k))
            landed(far_copies(k))

        pl.when(has_up)(up_landed)
        pl.when(has_down)(lambda: landed(up_copies(k)))

        def no_up():
            F[k, place(0)] = F[k, place(2)]
            F[k, place(1)] = F[k, place(2)]

        def no_down():
            F[k, place(6)] = F[k, place(5)]

        pl.when(jnp.logical_not(has_up))(no_up)
        pl.when(jnp.logical_not(has_down))(no_down)
        for q, (ahead, behind) in ((0, (0, 192)), (1, (64, 128)), (6, (128, 64))):
            at = pl.multiple_of(jnp.where(positive, ahead, behind), 64)
            before(place(q), Le[pl.ds(at, 64), :])
        upwind(1, False)
        upwind(2, True)
        upwind(5, True)
        Sf2[k] = moments(G[INNER : FACES - 2].reshape(WIDE, TILES * LANES))
        tail = G[FACES - 2 : FACES].reshape(16, TILES * LANES)
        tail = moments(jnp.concatenate([tail] * 8, axis=0))
        for h in range(2):
            Sf2[k, 13 + h : 14 + h, :LANES] = jnp.sum(
                jnp.where(lane // 16 == (8 - sub) % 8, tail[8 * h : 8 * h + 8], 0.0), axis=0, keepdims=True
            )
        start(face_copies(k, 1))

        target = F.at[1, 2:6] if k == 0 else O
        solid_rows(totc.at[k], kr[0:1, :], bound, CM, 256)
        expansion(CM, 256, Lm)
        for p in range(4):
            left = Lm[p * 64 : p * 64 + 64, :].astype(BF16)
            e = jnp.dot(left, TE[...], preferred_element_type=F32)
            a = jnp.dot(left, TA[...], preferred_element_type=F32)
            for t in range(TILES):
                cut = slice(t * LANES, (t + 1) * LANES)
                target[p, :, :, cut] = (a * jnp.exp2(e[:, cut])).reshape(8, 8, LANES)
            W[p] = (4.0 * B[p + 2, 1:7] - F[k, p + 2, 1:7]) * (1.0 / 3.0)

        for g, (sent, got, first, lines, block) in enumerate(
            ((Sf1, Rf1, 0, INNER, 8), (Sf2, Rf2, INNER, FACES - INNER, 10))
        ):
            landed(face_copies(k, g))
            sums = sent[k]
            for d in range(n_vel - 1):
                sums = sums + got[k, d]
            width = sums.shape[1]
            totf[:, :width] = sums
            if g:
                for h in range(2):
                    spread = jnp.broadcast_to(sums[13 + h : 14 + h, :LANES], (8, LANES))
                    totf[8 * h : 8 * h + 8, WIDE:] = pltpu.roll(
                        spread, 0, 1, stride=16, stride_axis=0
                    )
                width = WIDE + LANES
            target_rows(totf, width, C, HALF, False)
            expansion(C, width, Lf)
            size = block * 8
            for j in range(lines // block):
                at = first + j * block

                def get(t, at=at):
                    return G[at : at + block, :, t * LANES : (t + 1) * LANES].reshape(size, LANES)

                def put(t, value, at=at):
                    G[at : at + block, :, t * LANES : (t + 1) * LANES] = value.reshape(
                        block, 8, LANES
                    )

                relax(Lf[j * size : (j + 1) * size, :], get, put)

        for p in (3, 0, 2, 1):
            for y in range(1, 7):
                fluid = kb[p + 1, y] == 1.0
                for t in range(TILES):
                    cut = slice(t * LANES, (t + 1) * LANES)
                    z = G[Z_AT[p] + y - 1, :, cut]
                    change = (
                        xi_x[t // 2]
                        * (G[X_AT[p + 1] + y - 1, :, cut] - G[X_AT[p] + y - 1, :, cut])
                        + xi_y[t % 2] * (G[Y_AT[p] + y, :, cut] - G[Y_AT[p] + y - 1, :, cut])
                        + xi_z * (z - pltpu.roll(z, 1, 0))
                    )
                    fresh = W[p, y - 1, :, cut] - DT * change
                    target[p, y, :, cut] = jnp.where(fluid, fresh, target[p, y, :, cut])
            if k == STEPS - 1:
                pltpu.make_async_copy(O.at[p], out.at[p], out_sem.at[p]).start()
            elif p == 0:
                send_near(k + 1)
            elif p == 1:
                send_far(k + 1)

    one_step(0)
    send_cells(1)
    one_step(1)

    for k in range(STEPS):
        left_free(cell_copies(k))
        pl.when(s < last)(lambda k=k: left_free(right_copies(k)))
        pl.when(s > 0)(lambda k=k: left_free(left_copies(k)))
        pl.when(has_down)(lambda k=k: left_free(near_copies(k) + far_copies(k)))
        pl.when(has_up)(lambda k=k: left_free(up_copies(k)))
        for g in range(2):
            left_free(face_copies(k, g))
    for p in range(4):
        pltpu.make_async_copy(O.at[p], out.at[p], out_sem.at[p]).wait()


def solution(mesh):
    n_space, n_vel = mesh.shape["space"], mesh.shape["vel"]
    vmem, dma = pltpu.VMEM, pltpu.SemaphoreType.DMA
    width = TILES * LANES

    def on_device(dist, cell_type, boundary):
        peers = n_vel - 1
        return pl.pallas_call(
            functools.partial(kernel, n_space, n_vel),
            out_shape=jax.ShapeDtypeStruct(dist.shape, F32),
            in_specs=[
                pl.BlockSpec(memory_space=pltpu.HBM),
                pl.BlockSpec(memory_space=pltpu.HBM),
                pl.BlockSpec(memory_space=pl.ANY),
            ],
            out_specs=pl.BlockSpec(memory_space=pl.ANY),
            scratch_shapes=[
                vmem((2, 8, 8, 8, width), F32),
                vmem((8, 8, 8, width), F32),
                vmem((FACES, 8, width), F32),
                vmem((4, 6, 8, width), F32),
                vmem((4, 8, 8, width), F32),
                vmem((2, 16, 256), F32),
                vmem((2, peers, 16, 256), F32),
                vmem((2, 16, 128), F32),
                vmem((2, 16, 128), F32),
                vmem((2, 16, 256), F32),
                vmem((2, peers, 16, 256), F32),
                vmem((2, 16, WIDE), F32),
                vmem((2, peers, 16, WIDE), F32),
                vmem((2, 16, 256), F32),
                vmem((16, 256), F32),
                vmem((16, 512), F32),
                vmem((40, 512), F32),
                vmem((40, 256), F32),
                vmem((256, 128), F32),
                vmem((256, 128), F32),
                vmem((256, 128), F32),
                vmem((512, 128), F32),
                vmem((128, width), BF16),
                vmem((128, width), BF16),
                vmem((128, LANES), BF16),
                vmem((32, width), BF16),
                pltpu.SMEM((6,), F32),
                vmem((8, 8, LANES), jnp.int32),
                vmem((6, 8, 8, LANES), F32),
                vmem((8, 256), F32),
                dma,
                dma,
                dma,
                dma((4,)),
                dma((2, 3)),
                dma((2, 3)),
                dma((2, peers)),
                dma((2, peers)),
                dma((2,)),
                dma((2,)),
                dma((2,)),
                dma((2,)),
                dma((2, 2, peers)),
                dma((2, 2, peers)),
            ],
            compiler_params=pltpu.CompilerParams(
                collective_id=0, has_side_effects=True, vmem_limit_bytes=60 * 2**20
            ),
        )(dist, jnp.transpose(cell_type, (1, 2, 0)), boundary)

    return jax.shard_map(
        on_device,
        mesh=mesh,
        in_specs=(P("space", None, None, "vel"), P(), P()),
        out_specs=P("space", None, None, "vel"),
        check_vma=False,
    )
```
